512 devices in a mesh: dp: 64 (over y, z), tensor: 8 (over x, core).
Axes of the slice: x: 4, y: 4, z: 16, core: 2. Of those that a mesh axis runs over, the one named last changes fastest.
Arguments:
- context: bfloat16 [6144, 4096], P('dp', 'tensor'), may hold values from -0.25 to 0.25
- residual: bfloat16 [6144, 8192], P('tensor', 'dp'), may hold values from -300 to 300
- gain: float32 [8192], P('dp'), may hold values from 0.25 to 1.75
- start: float32 [4096, 8192], P('tensor', 'dp'), may hold values from -12 to 12
Outputs:
- basis: float32 [3, 4096, 8192], P(None, 'tensor', 'dp')
- alphas: float32 [2], replicated
- betas: float32 [2], replicated
The draws below stay inside these ranges and needn't reach their ends.
All inputs are finite; a program needn't handle non-finite values.
Results may differ from the reference program's by a relative error of at most 0.025.
Values may be sent and summed in bfloat16 or wider, within the bound.
A program may use at most 64 MiB of HBM per device.

```python
import jax
import jax.numpy as jnp
from jax import lax

D = 8192
ITERS = 2
CTX = 4096
TOKENS = 6144
N_TENSOR = 8


def draw_residual(key, part):
    key = jax.random.fold_in(key, 11)
    key_tok, key_col, key_noise = jax.random.split(key, 3)
    place = jnp.arange(D, dtype=jnp.float32) / D
    rough = jnp.exp(jax.random.uniform(key_col, (D,), jnp.float32, jnp.log(0.7), jnp.log(1.4)))
    ramp = 0.6 + 1.2 * place
    token_scale = jnp.exp(jax.random.uniform(key_tok, (TOKENS, 1), jnp.float32, 0.0, jnp.log(10.0)))
    noise = jnp.clip(0.8 * jax.random.normal(key_noise, (TOKENS, D), jnp.float32), -2.4, 2.4)
    values = token_scale * (ramp * rough)[None, :] * (1.0 + noise)
    return values.astype(jnp.bfloat16)


def draw_start(key, part):
    key = jax.random.fold_in(key, 13)
    key_rows, key_noise = jax.random.split(key, 2)
    place_col = jnp.arange(D, dtype=jnp.float32) / D
    place_row = jnp.arange(CTX, dtype=jnp.float32) / CTX
    row_ramp = 0.7 + 0.6 * place_row
    row_part = jnp.clip(jax.random.normal(key_rows, (CTX, 1), jnp.float32), -3.0, 3.0)
    col_ramp = 0.5 + place_col
    noise = jnp.clip(0.6 * jax.random.normal(key_noise, (CTX, D), jnp.float32), -1.8, 1.8)
    return (row_part + noise) * row_ramp[:, None] * col_ramp[None, :]


def steps_of(key, shape, shards, low, top_value):
    factor_of, own = 1.0, jax.random.fold_in(key, 6)
    for position, parts in shards:
        steps = jnp.exp(jax.random.uniform(jax.random.fold_in(own, position), (parts,), jnp.float32, low / len(shards), top_value / len(shards)))
        factor_of = factor_of * jnp.repeat(steps, shape[position] // parts).reshape([-1 if axis == position else 1 for axis in range(len(shape))])
    return factor_of


def normal_values(rng, dims, width, most, shards=(), kind=jnp.bfloat16):
    values = width * jax.random.normal(rng, dims, jnp.float32)
    if shards:
        values = values * steps_of(rng, dims, shards, -0.22, 0.18)
    return jnp.clip(values, -most, most).astype(kind)


def setup_inputs(seed: int = 0) -> dict:
    key_list = jax.random.split(jax.random.key(seed), 5)
    return {
        "context": normal_values(key_list[0], (TOKENS, CTX), (CTX ** -0.5), 0.25, ((0, 64), (1, 8))),
        "residual": draw_residual(jax.random.fold_in(key_list[4], 71), 0),
        "gain": jnp.clip(1.0 + 0.15 * jax.random.normal(key_list[2], (D,), jnp.float32), 0.25, 1.75),
        "start": draw_start(jax.random.fold_in(key_list[4], 71), 0),
    }


def reference(context, residual, gain, start):
    total = CTX * D
    block = CTX // N_TENSOR
    stream = residual.astype(jnp.float32)
    mean_sq = lax.optimization_barrier(jnp.sum(stream * stream, axis=1)) / D + 1e-06
    rms = jnp.sqrt(mean_sq)
    unit = stream / rms[:, None]
    gain_sq = gain * gain

    def product(vector):
        vec_b = vector.astype(jnp.bfloat16)
        summed = jnp.zeros((context.shape[0], D), jnp.float32)
        for index in range(N_TENSOR):
            partial_term = jnp.dot(context[:, index * block:(index + 1) * block], vec_b[index * block:(index + 1) * block], preferred_element_type=jnp.float32)
            summed = summed + partial_term.astype(jnp.bfloat16).astype(jnp.float32)
        change = lax.optimization_barrier(summed.astype(jnp.bfloat16)).astype(jnp.float32)
        along = lax.optimization_barrier(jnp.sum(unit * change, axis=1))
        scaled = gain_sq[None, :] * (change - unit * along[:, None] / D)
        back = lax.optimization_barrier(jnp.sum(unit * scaled, axis=1))
        err = ((scaled - unit * back[:, None] / D) / mean_sq[:, None]).astype(jnp.bfloat16)
        return lax.dot_general(context, err, (((0,), (0,)), ((), ())), preferred_element_type=jnp.float32)

    def inner(left, right):
        return jnp.sum(left * right) / total
    first = start / jnp.sqrt(inner(start, start) + 1e-06)
    vectors = [first]
    alpha_list = []
    beta_list = []
    for step in range(ITERS):
        image = product(vectors[step])
        coefs = [inner(older, image) for older in vectors]
        alpha_list.append(coefs[step])
        remain = image
        for older, coef in zip(vectors, coefs):
            remain = remain - coef * older
        beta = jnp.sqrt(inner(remain, remain) + 1e-06)
        beta_list.append(beta)
        vectors.append(remain / beta)
    return (jnp.stack(vectors), jnp.stack(alpha_list), jnp.stack(beta_list))
```

```python
import jax
import jax.numpy as jnp
from jax import lax
from jax.sharding import PartitionSpec as P

D = 8192
ITERS = 2
CTX = 4096
SCALE = 2.0 ** -20


def lanczos_coefs(g):
    total = float(CTX * D)
    g = [[g[i][j] / total for j in range(3)] for i in range(3)]

    def inner(a, b):
        return sum(a[i] * b[j] * g[i][j] for i in range(3) for j in range(3))

    def axpy(a, b, s):
        return [b[i] - s * a[i] for i in range(3)]

    zero = jnp.zeros((), jnp.float32)
    n0 = jnp.sqrt(g[0][0] + 1e-06)
    inv = 1.0 / n0
    q0 = [inv, zero, zero]
    w1 = [zero, inv / SCALE, zero]
    h00 = inner(q0, w1)
    r1 = axpy(q0, w1, h00)
    b0 = jnp.sqrt(jnp.maximum(inner(r1, r1), 0.0) + 1e-06)
    q1 = [x / b0 for x in r1]
    gw1 = [zero, zero, inv / SCALE / SCALE]
    w2 = [x / b0 for x in axpy(w1, gw1, h00)]
    h01 = inner(q0, w2)
    h11 = inner(q1, w2)
    r2 = axpy(q1, axpy(q0, w2, h01), h11)
    b1 = jnp.sqrt(jnp.maximum(inner(r2, r2), 0.0) + 1e-06)
    q2 = [x / b1 for x in r2]
    return q0, q1, q2, (h00, h11), (b0, b1)


def body(context, residual, gain, start):
    gathered = lax.all_gather(context, "dp", axis=0, tiled=True)
    gain_sq = gain * gain
    stream = residual.astype(jnp.float32)

    def psum_dp(x):
        return jnp.sum(lax.all_gather(x, "dp", axis=0, tiled=False), axis=0)

    sums = psum_dp(jnp.stack([jnp.sum(stream * stream, axis=1), jnp.sum(stream * stream * gain_sq[None, :], axis=1)]))
    mean_sq = sums[0] / D + 1e-06
    unit = stream / jnp.sqrt(mean_sq)[:, None]
    ugu = sums[1] / mean_sq
    vectors = [start]
    for step in range(ITERS):
        vec_b = vectors[step].astype(jnp.bfloat16)
        summed = lax.psum_scatter(
            jnp.dot(gathered, vec_b, preferred_element_type=jnp.float32).astype(jnp.bfloat16),
            "tensor",
            scatter_dimension=0,
            tiled=True,
        )
        change = summed.astype(jnp.float32)
        uc = unit * change
        both = psum_dp(jnp.stack([jnp.sum(uc, axis=1), jnp.sum(uc * gain_sq[None, :], axis=1)]))
        along = both[0]
        back = both[1] - along / D * ugu
        scaled = gain_sq[None, :] * (change - unit * along[:, None] / D)
        err = ((scaled - unit * back[:, None] / D) / mean_sq[:, None]).astype(jnp.bfloat16)
        image = lax.dot_general(
            gathered,
            lax.all_gather(err, "tensor", axis=0, tiled=True),
            (((0,), (0,)), ((), ())),
            preferred_element_type=jnp.float32,
        )
        vectors.append(image * SCALE)
    pairs = [(i, j) for i in range(3) for j in range(i, 3)]
    local = jnp.stack([jnp.sum(vectors[i] * vectors[j]) for i, j in pairs])
    gram = jnp.sum(lax.all_gather(local, ("dp", "tensor"), axis=0, tiled=False), axis=0)
    g = [[None] * 3 for _ in range(3)]
    for k, (i, j) in enumerate(pairs):
        g[i][j] = g[j][i] = gram[k]
    q0, q1, q2, alphas, betas = lanczos_coefs(g)
    basis = jnp.stack([sum(c[i] * vectors[i] for i in range(3)) for c in (q0, q1, q2)])
    return (basis, jnp.stack(alphas), jnp.stack(betas))


def solution(mesh):
    in_specs = (P("dp", "tensor"), P("tensor", "dp"), P("dp"), P("tensor", "dp"))
    out_specs = (P(None, "tensor", "dp"), P(), P())
    return jax.shard_map(body, mesh=mesh, in_specs=in_specs, out_specs=out_specs, check_vma=False)
```

```python
import functools

import jax
import jax.numpy as jnp
from jax import lax
from jax.experimental import pallas as pl
from jax.experimental.pallas import tpu as pltpu
from jax.sharding import PartitionSpec as P

ITERS = 2
SCALE = 2.0 ** -20
NX = 4
LB = 128
F32, BF16 = jnp.float32, jnp.bfloat16


def lanczos_coefs(g, total):
    g = [[g[i][j] / total for j in range(3)] for i in range(3)]

    def inner(a, b):
        return sum(a[i] * b[j] * g[i][j] for i in range(3) for j in range(3))

    def axpy(a, b, s):
        return [b[i] - s * a[i] for i in range(3)]

    zero = jnp.zeros_like(g[0][0])
    inv = 1.0 / jnp.sqrt(g[0][0] + 1e-06)
    q0 = [inv, zero, zero]
    w1 = [zero, inv / SCALE, zero]
    h00 = inner(q0, w1)
    r1 = axpy(q0, w1, h00)
    b0 = jnp.sqrt(jnp.maximum(inner(r1, r1), 0.0) + 1e-06)
    q1 = [v / b0 for v in r1]
    gw1 = [zero, zero, inv / SCALE / SCALE]
    w2 = [v / b0 for v in axpy(w1, gw1, h00)]
    h01 = inner(q0, w2)
    h11 = inner(q1, w2)
    r2 = axpy(q1, axpy(q0, w2, h01), h11)
    b1 = jnp.sqrt(jnp.maximum(inner(r2, r2), 0.0) + 1e-06)
    q2 = [v / b1 for v in r2]
    return (q0, q1, q2), (h00, h11), (b0, b1)


def kernel(cfg, ctx, res, gain, start, basis, ab, C, R, VT, UT, CT, TS, ER, WS, XR, TB, RR, W, PR, GR, send, recv, local):
    NZ, RU, FB, DB, D, CTX = cfg
    NT = NZ * 3 * RU
    RB = 3 * RU
    HALF = NZ // 2
    nrow = NT // LB
    i = lax.axis_index("dp")
    t = lax.axis_index("tensor")
    y, z = i // NZ, i % NZ
    x, c = t // 2, t % 2
    o = 1 - c

    def dev(X=None, Y=None, Z=None, K=None):
        X = x if X is None else X
        Y = y if Y is None else Y
        Z = z if Z is None else Z
        K = c if K is None else K
        return {"dp": Y * NZ + Z, "tensor": X * 2 + K}

    partner = dev(K=o)
    xs = [dev(X=(x + k) % NX) for k in (1, 2, 3)]
    ys = [dev(Y=(y + k) % NX) for k in (1, 2, 3)]
    right, left = dev(Z=(z + 1) % NZ), dev(Z=(z + NZ - 1) % NZ)
    za, zb = z // 4, z % 4
    NA = NZ // 4
    zbs = [dev(Z=za * 4 + (zb + k) % 4) for k in (1, 2, 3)]
    zas = [dev(Z=((za + k) % NA) * 4 + zb) for k in range(1, NA)]
    digits = {"x": (x, xs), "y": (y, ys), "b": (zb, zbs), "a": (za, zas), "c": (c, [partner])}

    count = [0]

    def xfer(src, dst, to):
        n = count[0]
        count[0] += 1
        copy = pltpu.make_async_remote_copy(
            src_ref=src, dst_ref=dst, send_sem=send.at[n], recv_sem=recv.at[n],
            device_id=to, device_id_type=pl.DeviceIdType.MESH,
        )
        return copy

    pending = []

    def go(src, dst, to):
        copy = xfer(src, dst, to)
        copy.start()
        pending.append(copy)
        return copy

    barrier = pltpu.get_barrier_semaphore()
    peers = [partner] + xs + ys + [right, left] + zbs + zas
    for p in peers:
        pl.semaphore_signal(barrier, 1, device_id=p, device_id_type=pl.DeviceIdType.MESH)

    @pl.when(x != y)
    def _():
        for k in (0, 1):
            pl.semaphore_signal(barrier, 1, device_id=dev(X=y, Y=x, K=k), device_id_type=pl.DeviceIdType.MESH)
        pl.semaphore_wait(barrier, len(peers) + 2)

    @pl.when(x == y)
    def _():
        pl.semaphore_wait(barrier, len(peers))

    own_rows = pl.ds(pl.multiple_of(z * RB, RU), RB)
    fcol = pl.ds(pl.multiple_of(y * FB, FB), FB)
    scol = pl.ds(pl.multiple_of(x * FB, FB), FB)
    same = xfer(ctx.at[pl.ds(pl.multiple_of(c * RB, RU), RB)], C.at[c, own_rows, scol], dev(X=y, Y=x))
    keep = pltpu.make_async_copy(ctx.at[pl.ds(pl.multiple_of(c * RB, RU), RB)], C.at[c, own_rows, scol], local.at[0])

    @pl.when(x != y)
    def _():
        same.start()

    @pl.when(x == y)
    def _():
        keep.start()

    other = go(ctx.at[pl.ds(pl.multiple_of(o * RB, RU), RB)], C.at[c, own_rows, scol], dev(X=y, Y=x, K=o))

    rmine = pltpu.make_async_copy(
        res.at[:, pl.ds(pl.multiple_of(c * RB, RU), RB)], R.at[pl.ds(c * HALF, HALF)], local.at[1])
    rmine.start()
    rswap = go(res.at[:, pl.ds(pl.multiple_of(o * RB, RU), RB)], R.at[pl.ds(c * HALF, HALF)], partner)

    mine = pl.ds(pl.multiple_of(x * FB, FB), FB)

    def gather_vector(slot):
        out = [go(VT.at[slot, c, :, mine], VT.at[slot, c, :, mine], p) for p in xs]
        back = [go(VT.at[slot, c, :, mine], VT.at[slot, c, :, mine], partner)]
        return out, back

    def forward_vector(slot, out, back):
        for k, copy in zip((1, 2, 3), out):
            copy.wait_recv()
            blk = pl.ds(pl.multiple_of(((x + NX - k) % NX) * FB, FB), FB)
            back.append(go(VT.at[slot, c, :, blk], VT.at[slot, c, :, blk], partner))

    st = start[...].T
    W[0] = st
    VT[0, c, :, mine] = st.astype(BF16)
    vout, vback = gather_vector(0)

    @pl.when(x != y)
    def _():
        same.wait()

    @pl.when(x == y)
    def _():
        keep.wait()

    other.wait_recv()

    def third(zz):
        return pl.ds(pl.multiple_of(zz * RB, RU), RU)

    def rest(zz):
        return pl.ds(pl.multiple_of(zz * RB + RU, RU), 2 * RU)

    def rest_of(zz, h):
        return pl.ds(pl.multiple_of(zz * RB + RU + h * RU, RU), RU)

    def send_third(zz, to):
        return go(C.at[:, third(zz)], C.at[:, third(zz)], to)

    def send_rest(zz, to):
        return go(C.at[:, rest(zz), fcol], C.at[:, rest(zz), fcol], to)

    def ycopies(zz):
        return [send_rest(zz, ys[0]), send_rest(zz, ys[2])]

    def yforward(zz, copies):
        down = pl.ds(pl.multiple_of(((y + NX - 1) % NX) * FB, FB), FB)
        up = pl.ds(pl.multiple_of(((y + 1) % NX) * FB, FB), FB)
        copies[0].wait_recv()
        a = go(C.at[:, rest_of(zz, 0), down], C.at[:, rest_of(zz, 0), down], ys[0])
        copies[1].wait_recv()
        b = go(C.at[:, rest_of(zz, 1), up], C.at[:, rest_of(zz, 1), up], ys[2])
        return [a, b]

    last = []
    r2, l2 = send_rest(z, right), send_rest(z, left)
    y1 = [go(C.at[:, third(z), fcol], C.at[:, third(z), fcol], p) for p in ys]
    yq = [(z, ycopies(z))]
    for copy in y1:
        copy.wait_recv()
    r1, l1 = send_third(z, right), send_third(z, left)

    def reduce_stage(buf, dig):
        me, ps = digits[dig]
        return [go(buf.at[me], buf.at[me], p) for p in ps]

    def finish_stage(buf, dig, copies):
        for copy in copies:
            copy.wait_recv()
        n = len(copies) + 1
        total = buf[0]
        for k in range(1, n):
            total = total + buf[k]
        return total

    stages = [s for s in ("y", "b", "a") if len(digits[s][1])]

    def pack(ref, a1, a2):
        for j in range(nrow):
            ref[j:j + 1, :] = a1[:, j * LB:(j + 1) * LB]
            ref[8 + j:9 + j, :] = a2[:, j * LB:(j + 1) * LB]

    def unpack(v):
        return (jnp.concatenate([v[j:j + 1] for j in range(nrow)], axis=1),
                jnp.concatenate([v[8 + j:9 + j] for j in range(nrow)], axis=1))

    def dp_sum_steps(call, a1, a2):
        me = digits[stages[0]][0]
        PR[call, 0, me] = jnp.zeros((16, LB), F32)
        pack(PR.at[call, 0, me], a1, a2)
        for s, dig in enumerate(stages):
            copies = reduce_stage(PR.at[call, s], dig)
            yield None
            v = finish_stage(PR.at[call, s], dig, copies)
            if s + 1 < len(stages):
                PR[call, s + 1, digits[stages[s + 1]][0]] = v
        yield unpack(v)

    gsq = gain[...] * gain[...]
    g2 = jnp.broadcast_to(gsq, (DB, DB)).T[:, 0:1]

    def setup():
        rmine.wait()
        rswap.wait_recv()
        rt = R[...].reshape(NT, DB).astype(F32).T
        UT[...] = rt
        sq = rt * rt
        steps = dp_sum_steps(0, jnp.sum(sq, axis=0, keepdims=True), jnp.sum(sq * g2, axis=0, keepdims=True))
        for v in steps:
            if v is None:
                yield
        ms = v[0] / D + 1e-06
        UT[...] = UT[...] / jnp.sqrt(ms)
        TS[0:1, :] = v[1] / ms
        TS[1:2, :] = 1.0 / ms

    side = setup()
    yq2 = []
    for s in range(1, HALF + 1):
        zr, zl = (z + NZ - s) % NZ, (z + s) % NZ
        r2.wait_recv()
        if s < HALF:
            r2 = send_rest(zr, right)
        r1.wait_recv()
        if s < HALF:
            r1 = send_third(zr, right)
        new = [(zr, ycopies(zr))]
        if s < NZ - HALF:
            l2.wait_recv()
            if s < NZ - HALF - 1:
                l2 = send_rest(zl, left)
            l1.wait_recv()
            if s < NZ - HALF - 1:
                l1 = send_third(zl, left)
            new.append((zl, ycopies(zl)))
        for zz, copies in yq:
            last += yforward(zz, copies)
        yq = new
        if s == 1:
            forward_vector(0, vout, vback)
        next(side, None)
    for zz, copies in yq:
        last += yforward(zz, copies)
    for _ in side:
        pass
    for copy in vback + last:
        copy.wait_recv()

    MB = NT // 2
    for step in range(ITERS):
        def rows(m, carry, step=step):
            r = pl.ds(pl.multiple_of(m * MB, LB), MB)
            acc = lax.dot_general(C[0, r, :], VT[step, 0], (((1,), (1,)), ((), ())), preferred_element_type=F32)
            acc += lax.dot_general(C[1, r, :], VT[step, 1], (((1,), (1,)), ((), ())), preferred_element_type=F32)
            CT[:, r] = acc.T
            return carry

        lax.fori_loop(0, 2, rows, 0)
        uc = UT[...] * CT[...]
        for v in dp_sum_steps(1 + step, jnp.sum(uc, axis=0, keepdims=True), jnp.sum(uc * g2, axis=0, keepdims=True)):
            pass
        along = v[0] / D
        back = v[1] / D - along * TS[0:1, :] / D
        ut = UT[...]
        ER[...] = ((g2 * (CT[...] - ut * along) - ut * back) * TS[1:2, :]).astype(BF16)

        swaps = []
        for X in range(NX):
            col = slice(X * FB, (X + 1) * FB)
            WS[step, :, col] = jnp.dot(ER[...], C[o, :, col], preferred_element_type=F32).astype(BF16)
            swaps.append(go(WS.at[step, :, col], XR.at[step, :, col], partner))
        sums = []
        for k in (1, 2, 3, 0):
            X = (x + k) % NX
            col = pl.ds(pl.multiple_of(X * FB, FB), FB)
            TB[k] = jnp.dot(ER[...], C[c, :, col], preferred_element_type=F32)
        for copy in swaps:
            copy.wait_recv()
        for k in (1, 2, 3):
            X = (x + k) % NX
            col = pl.ds(pl.multiple_of(X * FB, FB), FB)
            RR[step, 3 + k] = (TB[k] + XR[step, :, col].astype(F32)).astype(BF16)
            sums.append(go(RR.at[step, 3 + k], RR.at[step, k], xs[k - 1]))
        total = TB[0] + XR[step, :, mine].astype(F32)
        for k, copy in zip((1, 2, 3), sums):
            copy.wait_recv()
            total = total + RR[step, k].astype(F32)
        total = total * SCALE
        W[step + 1] = total
        if step + 1 < ITERS:
            VT[step + 1, c, :, mine] = total.astype(BF16)
            vout, vback = gather_vector(step + 1)
            forward_vector(step + 1, vout, vback)
            for copy in vback:
                copy.wait_recv()

    pairs = [(a, b) for a in range(3) for b in range(a, 3)]
    order = ["c", "x"] + stages
    GR[0, c] = jnp.zeros((8, LB), F32)
    for n, (a, b) in enumerate(pairs):
        prod = jnp.sum(W[a] * W[b], axis=0, keepdims=True)
        GR[0, c, n:n + 1, :] = functools.reduce(
            lambda p, q: p + q, [prod[:, j * LB:(j + 1) * LB] for j in range(FB // LB)])
    for s, dig in enumerate(order):
        v = finish_stage(GR.at[s], dig, reduce_stage(GR.at[s], dig))
        if s + 1 < len(order):
            GR[s + 1, digits[order[s + 1]][0]] = v
    v = jnp.sum(v, axis=1, keepdims=True)
    g = [[None] * 3 for _ in range(3)]
    for n, (a, b) in enumerate(pairs):
        g[a][b] = g[b][a] = v[n:n + 1]
    qs, alphas, betas = lanczos_coefs(g, float(CTX * D))
    for n, q in enumerate(qs):
        basis[n] = sum(q[k] * W[k] for k in range(n + 1)).T
    for n, value in enumerate(alphas + betas):
        ab[n:n + 1, :] = jnp.broadcast_to(value, (1, LB))
    ab[4:8, :] = jnp.zeros((4, LB), F32)
    for copy in pending:
        copy.wait_send()


def body(cfg, context, residual, gain, start):
    NZ, RU, FB, DB, D, CTX = cfg
    NT, RB = NZ * 3 * RU, 3 * RU
    vmem = pl.BlockSpec(memory_space=pltpu.VMEM)
    flops = 8 * NT * CTX * DB
    basis, ab = pl.pallas_call(
        functools.partial(kernel, cfg),
        out_shape=(jax.ShapeDtypeStruct((3, FB, DB), F32), jax.ShapeDtypeStruct((8, LB), F32)),
        in_specs=[vmem] * 4,
        out_specs=(vmem, vmem),
        scratch_shapes=[
            pltpu.VMEM((2, NT, NX * FB), BF16),
            pltpu.VMEM((NZ, RB, DB), BF16),
            pltpu.VMEM((ITERS, 2, DB, NX * FB), BF16),
            pltpu.VMEM((DB, NT), F32),
            pltpu.VMEM((DB, NT), F32),
            pltpu.VMEM((8, NT), F32),
            pltpu.VMEM((DB, NT), BF16),
            pltpu.VMEM((ITERS, DB, NX * FB), BF16),
            pltpu.VMEM((ITERS, DB, NX * FB), BF16),
            pltpu.VMEM((4, DB, FB), F32),
            pltpu.VMEM((ITERS, 7, DB, FB), BF16),
            pltpu.VMEM((3, DB, FB), F32),
            pltpu.VMEM((ITERS + 1, 3, 4, 16, LB), F32),
            pltpu.VMEM((5, 4, 8, LB), F32),
            pltpu.SemaphoreType.DMA((256,)),
            pltpu.SemaphoreType.DMA((256,)),
            pltpu.SemaphoreType.DMA((2,)),
        ],
        compiler_params=pltpu.CompilerParams(collective_id=0, has_side_effects=True, vmem_limit_bytes=40 * 2 ** 20),
        cost_estimate=pl.CostEstimate(flops=flops, bytes_accessed=2 ** 21, transcendentals=0),
    )(context, residual.reshape(NZ // 2, 2 * RB, DB), gain.reshape(1, DB), start)
    return basis, ab[0:2, 0], ab[2:4, 0]


def solution(mesh):
    cfg = (16, 16, 512, 128, 8192, 4096)
    in_specs = (P("dp", "tensor"), P("tensor", "dp"), P("dp"), P("tensor", "dp"))
    out_specs = (P(None, "tensor", "dp"), P(), P())
    return jax.shard_map(
        functools.partial(body, cfg), mesh=mesh, in_specs=in_specs, out_specs=out_specs, check_vma=False)
```

```python
import functools

import jax
import jax.numpy as jnp
from jax import lax
from jax.experimental import pallas as pl
from jax.experimental.pallas import tpu as pltpu
from jax.sharding import PartitionSpec as P

ITERS = 2
SCALE = 2.0 ** -20
NX = 4
LB = 128
F32, BF16 = jnp.float32, jnp.bfloat16


def lanczos_coefs(g, total):
    g = [[g[i][j] / total for j in range(3)] for i in range(3)]

    def inner(a, b):
        return sum(a[i] * b[j] * g[i][j] for i in range(3) for j in range(3))

    def axpy(a, b, s):
        return [b[i] - s * a[i] for i in range(3)]

    zero = jnp.zeros_like(g[0][0])
    inv = 1.0 / jnp.sqrt(g[0][0] + 1e-06)
    q0 = [inv, zero, zero]
    w1 = [zero, inv / SCALE, zero]
    h00 = inner(q0, w1)
    r1 = axpy(q0, w1, h00)
    b0 = jnp.sqrt(jnp.maximum(inner(r1, r1), 0.0) + 1e-06)
    q1 = [v / b0 for v in r1]
    gw1 = [zero, zero, inv / SCALE / SCALE]
    w2 = [v / b0 for v in axpy(w1, gw1, h00)]
    h01 = inner(q0, w2)
    h11 = inner(q1, w2)
    r2 = axpy(q1, axpy(q0, w2, h01), h11)
    b1 = jnp.sqrt(jnp.maximum(inner(r2, r2), 0.0) + 1e-06)
    q2 = [v / b1 for v in r2]
    return (q0, q1, q2), (h00, h11), (b0, b1)


def kernel(cfg, ctx, res, gain, start, basis, ab, C, R, ST, GN, VT, UT, CT, TS, ER, WS, XR, TB, RR, W, P1, P2, GC, GX, GZ, send, recv, local):
    NZ, RU, FB, DB, D, CTX = cfg
    NT = NZ * 3 * RU
    RB = 3 * RU
    HALF = NZ // 2
    nrow = NT // LB
    i = lax.axis_index("dp")
    t = lax.axis_index("tensor")
    y, z = i // NZ, i % NZ
    x, c = t // 2, t % 2
    o = 1 - c

    def dev(dx=0, dy=0, dz=0, core=None):
        return {
            "dp": ((y + dy) % NX) * NZ + (z + dz) % NZ,
            "tensor": ((x + dx) % NX) * 2 + (c if core is None else core),
        }

    def turned(core):
        return {"dp": x * NZ + z, "tensor": y * 2 + core}

    partner = dev(core=o)
    xs = [dev(dx=k) for k in (1, 2, 3)]
    ys = [dev(dy=k) for k in (1, 2, 3)]
    right, left = dev(dz=1), dev(dz=NZ - 1)

    count = [0]
    pending = []

    def xfer(src, dst, to):
        n = count[0]
        count[0] += 1
        return pltpu.make_async_remote_copy(
            src_ref=src, dst_ref=dst, send_sem=send.at[n], recv_sem=recv.at[n],
            device_id=to, device_id_type=pl.DeviceIdType.MESH,
        )

    def go(src, dst, to):
        copy = xfer(src, dst, to)
        copy.start()
        pending.append(copy)
        return copy

    def signal(to):
        pl.semaphore_signal(barrier, 1, device_id=to, device_id_type=pl.DeviceIdType.MESH)

    barrier = pltpu.get_barrier_semaphore()
    near = [partner] + xs + ys + [right, left]
    for p in near:
        signal(p)

    @pl.when(x != y)
    def _():
        signal(turned(0))
        signal(turned(1))

    own_rows = pl.ds(pl.multiple_of(z * RB, RU), RB)
    fcol = pl.ds(pl.multiple_of(y * FB, FB), FB)
    mine = pl.ds(pl.multiple_of(x * FB, FB), FB)
    half = [pl.ds(pl.multiple_of(k * RB, RU), RB) for k in (c, o)]
    getst = pltpu.make_async_copy(start, ST, local.at[2])
    getst.start()
    getgn = pltpu.make_async_copy(gain, GN, local.at[3])
    getgn.start()
    rmine = pltpu.make_async_copy(res.at[:, half[0]], R.at[pl.ds(c * HALF, HALF)], local.at[1])
    rmine.start()
    keep = pltpu.make_async_copy(ctx.at[half[0]], C.at[c, own_rows, mine], local.at[0])

    @pl.when(x == y)
    def _():
        keep.start()

    getst.wait()
    st = ST[...].T
    W[0] = st
    VT[0, c, :, mine] = st.astype(BF16)

    @pl.when(x != y)
    def _():
        pl.semaphore_wait(barrier, len(near) + 2)

    @pl.when(x == y)
    def _():
        pl.semaphore_wait(barrier, len(near))

    same = xfer(ctx.at[half[0]], C.at[c, own_rows, mine], turned(c))

    @pl.when(x != y)
    def _():
        same.start()

    other = go(ctx.at[half[1]], C.at[c, own_rows, mine], turned(o))

    def gather_vector(slot):
        out = [go(VT.at[slot, c, :, mine], VT.at[slot, c, :, mine], p) for p in xs]
        back = [go(VT.at[slot, c, :, mine], VT.at[slot, c, :, mine], partner)]
        return out, back

    def forward_vector(slot, out, back):
        for k in (1, 3, 2):
            out[k - 1].wait_recv()
            blk = pl.ds(pl.multiple_of(((x + NX - k) % NX) * FB, FB), FB)
            back.append(go(VT.at[slot, c, :, blk], VT.at[slot, c, :, blk], partner))

    vout, vback = gather_vector(0)
    rswap = go(res.at[:, half[1]], R.at[pl.ds(c * HALF, HALF)], partner)

    @pl.when(x != y)
    def _():
        same.wait()

    @pl.when(x == y)
    def _():
        keep.wait()

    other.wait_recv()

    def third(zz):
        return pl.ds(pl.multiple_of(zz * RB, RU), RU)

    def rest(zz):
        return pl.ds(pl.multiple_of(zz * RB + RU, RU), 2 * RU)

    def rest_of(zz, h):
        return pl.ds(pl.multiple_of(zz * RB + RU + h * RU, RU), RU)

    def send_third(h, zz, to):
        return go(C.at[h, third(zz)], C.at[h, third(zz)], to)

    def send_rest(zz, to):
        return go(C.at[:, rest(zz), fcol], C.at[:, rest(zz), fcol], to)

    def send_rest_half(h, zz, to):
        return go(C.at[h, rest(zz), fcol], C.at[h, rest(zz), fcol], to)

    def ycopies(zz):
        return zz, send_rest(zz, ys[0]), send_rest(zz, ys[2])

    last = []

    def yforward(item):
        zz, up, down = item
        below = pl.ds(pl.multiple_of(((y + NX - 1) % NX) * FB, FB), FB)
        above = pl.ds(pl.multiple_of(((y + 1) % NX) * FB, FB), FB)
        up.wait_recv()
        last.append(go(C.at[:, rest_of(zz, 0), below], C.at[:, rest_of(zz, 0), below], ys[0]))
        down.wait_recv()
        last.append(go(C.at[:, rest_of(zz, 1), above], C.at[:, rest_of(zz, 1), above], ys[2]))

    first = [dev(dy=a, dz=b) for b in (1, 0) for a in (2, 1, 3, 0) if a or b]
    second = [dev(dz=(HALF + k) % NZ) for k in sorted(range(0, NZ, 2), key=lambda v: min(v, NZ - v)) if (HALF + k) % NZ]

    def fan(buf, call, peers):
        return [go(buf.at[call, 0], buf.at[call, k + 1], p) for k, p in enumerate(peers)]

    def add_up(buf, call, copies):
        total = buf[call, 0]
        for k, copy in reversed(list(enumerate(copies))):
            copy.wait_recv()
            total = total + buf[call, k + 1]
        return total

    def fan_first(call, a1, a2):
        for j in range(nrow):
            P1[call, 0, j:j + 1, :] = a1[:, j * LB:(j + 1) * LB]
            P1[call, 0, nrow + j:nrow + j + 1, :] = a2[:, j * LB:(j + 1) * LB]
        return fan(P1, call, first)

    def fan_second(call, copies):
        P2[call, 0] = add_up(P1, call, copies)
        return fan(P2, call, second)

    def finish(call, copies):
        v = add_up(P2, call, copies)
        return (jnp.concatenate([v[j:j + 1] for j in range(nrow)], axis=1),
                jnp.concatenate([v[nrow + j:nrow + j + 1] for j in range(nrow)], axis=1))

    ar, al = send_rest(z, right), send_rest(z, left)
    y1 = [go(C.at[:, third(z), fcol], C.at[:, third(z), fcol], p) for p in ys]
    queue = [[], [ycopies(z)]]
    for copy in y1:
        copy.wait_recv()
    br, bl = [None, None], [None, None]
    for h in (0, 1):
        br[h], bl[h] = send_third(h, z, right), send_third(h, z, left)

    getgn.wait()
    gsq = GN[...] * GN[...]
    g2 = jnp.broadcast_to(gsq, (DB, DB)).T[:, 0:1]

    for s in range(1, HALF + 1):
        zr, zl = (z + NZ - s) % NZ, (z + s) % NZ
        end = s == HALF
        ar.wait_recv()
        if s < HALF - 1:
            ar = send_rest(zr, right)
        elif not end:
            ar = send_rest_half(0, zr, right)
        al.wait_recv()
        if s < HALF - 1:
            al = send_rest(zl, left)
        elif not end:
            al = send_rest_half(1, zl, left)
        now = [ycopies(zr)] if end else [ycopies(zr), ycopies(zl)]
        for h in (0, 1):
            if not end or h == 0:
                br[h].wait_recv()
            if s < HALF - 1 or (not end and h == 0):
                br[h] = send_third(h, zr, right)
            if not end or h == 1:
                bl[h].wait_recv()
            if s < HALF - 1 or (not end and h == 1):
                bl[h] = send_third(h, zl, left)
        queue.append(now)
        for item in queue.pop(0):
            yforward(item)
        if s == 1:
            forward_vector(0, vout, vback)
        if s == 2:
            rmine.wait()
            rswap.wait_recv()
            rt = R[...].reshape(NT, DB).astype(F32).T
            UT[...] = rt
            sq = rt * rt
            sums0 = fan_first(0, jnp.sum(sq, axis=0, keepdims=True), jnp.sum(sq * g2, axis=0, keepdims=True))
    sums0 = fan_second(0, sums0)
    for items in queue:
        for item in items:
            yforward(item)
    for copy in vback + last:
        copy.wait_recv()

    MB = NT // 2
    pairs = [(a, b) for b in range(3) for a in range(b + 1)]
    zeros = jnp.zeros((8, LB), F32)

    def gram_rows(b):
        for n, (p, q) in enumerate(pairs):
            if q == b:
                prod = jnp.sum(W[p] * W[q], axis=0, keepdims=True)
                GC[0, n:n + 1, :] = functools.reduce(
                    lambda m, v: m + v, [prod[:, j * LB:(j + 1) * LB] for j in range(FB // LB)])

    GC[0] = zeros
    for step in range(ITERS):
        def rows(m, carry, step=step):
            r = pl.ds(pl.multiple_of(m * MB, LB), MB)
            acc = lax.dot_general(C[0, r, :], VT[step, 0], (((1,), (1,)), ((), ())), preferred_element_type=F32)
            acc += lax.dot_general(C[1, r, :], VT[step, 1], (((1,), (1,)), ((), ())), preferred_element_type=F32)
            CT[:, r] = acc.T
            return carry

        lax.fori_loop(0, 2, rows, 0)
        uc = UT[...] * CT[...]
        sums = fan_first(1 + step, jnp.sum(uc, axis=0, keepdims=True), jnp.sum(uc * g2, axis=0, keepdims=True))
        if step == 0:
            s1, s2 = finish(0, sums0)
            ms = s1 / D + 1e-06
            TS[0:1, :] = 1.0 / ms
            TS[1:2, :] = 1.0 / jnp.sqrt(ms)
            TS[2:3, :] = s2 / ms
        sums = fan_second(1 + step, sums)
        gram_rows(step)
        a1, a2 = finish(1 + step, sums)
        ims, irms = TS[0:1, :], TS[1:2, :]
        along = a1 * irms / D
        back = a2 * irms / D - along * (TS[2:3, :] / D)
        ER[...] = ((g2 * (CT[...] - UT[...] * (irms * along)) - UT[...] * (irms * back)) * ims).astype(BF16)

        swaps, outs = {}, {}

        def swap(k):
            col = pl.ds(pl.multiple_of(((x + k) % NX) * FB, FB), FB)
            WS[step, :, col] = jnp.dot(ER[...], C[o, :, col], preferred_element_type=F32).astype(BF16)
            swaps[k] = go(WS.at[step, :, col], XR.at[step, :, col], partner)
            TB[k] = jnp.dot(ER[...], C[c, :, col], preferred_element_type=F32)

        def out(k):
            col = pl.ds(pl.multiple_of(((x + k) % NX) * FB, FB), FB)
            swaps[k].wait_recv()
            total = TB[k] + XR[step, :, col].astype(F32)
            if k:
                RR[step, 3 + k] = total.astype(BF16)
                outs[k] = go(RR.at[step, 3 + k], RR.at[step, k], xs[k - 1])
            return total

        order = (2, 1, 3, 0)
        swap(order[0])
        for n in (1, 2, 3):
            swap(order[n])
            out(order[n - 1])
        total = out(0)
        for k in (1, 3, 2):
            outs[k].wait_recv()
            total = total + RR[step, k].astype(F32)
        total = total * SCALE
        W[step + 1] = total
        if step + 1 < ITERS:
            VT[step + 1, c, :, mine] = total.astype(BF16)
            vout, vback = gather_vector(step + 1)
            forward_vector(step + 1, vout, vback)
            for copy in vback:
                copy.wait_recv()

    gram_rows(2)
    copy = go(GC.at[0], GC.at[1], partner)
    copy.wait_recv()
    xy = x * NX + y
    GX[xy] = GC[0] + GC[1]
    copies = [go(GX.at[xy], GX.at[xy], dev(dx=a, dy=b)) for a in (2, 1, 3, 0) for b in (2, 1, 3, 0) if a or b]
    for copy in copies:
        copy.wait_recv()
    v = functools.reduce(lambda m, w: m + w, [GX[k] for k in range(NX * NX)])
    v = jnp.sum(v, axis=1, keepdims=True)
    lane = lax.broadcasted_iota(jnp.int32, (8, LB), 1)
    GZ[z] = jnp.sum(jnp.where(lane == lax.broadcasted_iota(jnp.int32, (8, LB), 0), v, 0.0), axis=0, keepdims=True)
    far = sorted(range(1, NZ), key=lambda k: -min(k, NZ - k))
    copies = [go(GZ.at[z], GZ.at[z], dev(dz=k)) for k in far]
    for copy in copies:
        copy.wait_recv()
    v = functools.reduce(lambda m, w: m + w, [GZ[k] for k in range(NZ)])
    g = [[None] * 3 for _ in range(3)]
    for n, (a, b) in enumerate(pairs):
        g[a][b] = g[b][a] = jnp.sum(jnp.where(lane[0:1] == n, v, 0.0), axis=1, keepdims=True)
    qs, alphas, betas = lanczos_coefs(g, float(CTX * D))
    for n, q in enumerate(qs):
        basis[n] = sum(q[k] * W[k] for k in range(n + 1)).T
    for n, value in enumerate(alphas + betas):
        ab[n:n + 1, :] = jnp.broadcast_to(value, (1, LB))
    ab[4:8, :] = jnp.zeros((4, LB), F32)
    for copy in pending:
        copy.wait_send()


def body(cfg, context, residual, gain, start):
    NZ, RU, FB, DB, D, CTX = cfg
    NT, RB = NZ * 3 * RU, 3 * RU
    vmem = pl.BlockSpec(memory_space=pltpu.VMEM)
    flops = 8 * NT * CTX * DB
    basis, ab = pl.pallas_call(
        functools.partial(kernel, cfg),
        out_shape=(jax.ShapeDtypeStruct((3, FB, DB), F32), jax.ShapeDtypeStruct((8, LB), F32)),
        in_specs=[pl.BlockSpec(memory_space=pltpu.HBM)] * 4,
        out_specs=(vmem, vmem),
        scratch_shapes=[
            pltpu.VMEM((2, NT, NX * FB), BF16),
            pltpu.VMEM((NZ, RB, DB), BF16),
            pltpu.VMEM((FB, DB), F32),
            pltpu.VMEM((1, DB), F32),
            pltpu.VMEM((ITERS, 2, DB, NX * FB), BF16),
            pltpu.VMEM((DB, NT), F32),
            pltpu.VMEM((DB, NT), F32),
            pltpu.VMEM((8, NT), F32),
            pltpu.VMEM((DB, NT), BF16),
            pltpu.VMEM((ITERS, DB, NX * FB), BF16),
            pltpu.VMEM((ITERS, DB, NX * FB), BF16),
            pltpu.VMEM((4, DB, FB), F32),
            pltpu.VMEM((ITERS, 7, DB, FB), BF16),
            pltpu.VMEM((3, DB, FB), F32),
            pltpu.VMEM((ITERS + 1, 8, 2 * (NT // LB), LB), F32),
            pltpu.VMEM((ITERS + 1, NZ // 2, 2 * (NT // LB), LB), F32),
            pltpu.VMEM((2, 8, LB), F32),
            pltpu.VMEM((NX * NX, 8, LB), F32),
            pltpu.VMEM((NZ, 1, LB), F32),
            pltpu.SemaphoreType.DMA((320,)),
            pltpu.SemaphoreType.DMA((320,)),
            pltpu.SemaphoreType.DMA((4,)),
        ],
        compiler_params=pltpu.CompilerParams(collective_id=0, has_side_effects=True, vmem_limit_bytes=40 * 2 ** 20),
        cost_estimate=pl.CostEstimate(flops=flops, bytes_accessed=2 ** 21, transcendentals=0),
    )(context, residual.reshape(NZ // 2, 2 * RB, DB), gain.reshape(1, DB), start)
    return basis, ab[0:2, 0], ab[2:4, 0]


def solution(mesh):
    cfg = (16, 16, 512, 128, 8192, 4096)
    in_specs = (P("dp", "tensor"), P("tensor", "dp"), P("dp"), P("tensor", "dp"))
    out_specs = (P(None, "tensor", "dp"), P(), P())
    return jax.shard_map(
        functools.partial(body, cfg), mesh=mesh, in_specs=in_specs, out_specs=out_specs, check_vma=False)
```

```python
import functools

import jax
import jax.numpy as jnp
from jax import lax
from jax.experimental import pallas as pl
from jax.experimental.pallas import tpu as pltpu
from jax.sharding import PartitionSpec as P

ITERS = 2
SCALE = 2.0 ** -20
NX = 4
LB = 128
F32, BF16 = jnp.float32, jnp.bfloat16


def lanczos_coefs(g, total):
    g = [[g[i][j] / total for j in range(3)] for i in range(3)]

    def inner(a, b):
        return sum(a[i] * b[j] * g[i][j] for i in range(3) for j in range(3))

    def axpy(a, b, s):
        return [b[i] - s * a[i] for i in range(3)]

    zero = jnp.zeros_like(g[0][0])
    inv = 1.0 / jnp.sqrt(g[0][0] + 1e-06)
    q0 = [inv, zero, zero]
    w1 = [zero, inv / SCALE, zero]
    h00 = inner(q0, w1)
    r1 = axpy(q0, w1, h00)
    b0 = jnp.sqrt(jnp.maximum(inner(r1, r1), 0.0) + 1e-06)
    q1 = [v / b0 for v in r1]
    gw1 = [zero, zero, inv / SCALE / SCALE]
    w2 = [v / b0 for v in axpy(w1, gw1, h00)]
    h01 = inner(q0, w2)
    h11 = inner(q1, w2)
    r2 = axpy(q1, axpy(q0, w2, h01), h11)
    b1 = jnp.sqrt(jnp.maximum(inner(r2, r2), 0.0) + 1e-06)
    q2 = [v / b1 for v in r2]
    return (q0, q1, q2), (h00, h11), (b0, b1)


def kernel(cfg, ctx, res, gain, start, basis, ab, C, R, ST, GN, VT, UT, CT, AC, TS, ER, WS, XR, TB, RR, W, P1, P2, GC, GX, GZ, send, recv, local):
    NZ, RU, FB, DB, D, CTX = cfg
    NT = NZ * 3 * RU
    RB = 3 * RU
    HALF = NZ // 2
    nrow = NT // LB
    i = lax.axis_index("dp")
    t = lax.axis_index("tensor")
    y, z = i // NZ, i % NZ
    x, c = t // 2, t % 2
    o = 1 - c

    def dev(dx=0, dy=0, dz=0, core=None):
        return {
            "dp": ((y + dy) % NX) * NZ + (z + dz) % NZ,
            "tensor": ((x + dx) % NX) * 2 + (c if core is None else core),
        }

    def turned(core):
        return {"dp": x * NZ + z, "tensor": y * 2 + core}

    partner = dev(core=o)
    xs = [dev(dx=k) for k in (1, 2, 3)]
    ys = [dev(dy=k) for k in (1, 2, 3)]
    right, left = dev(dz=1), dev(dz=NZ - 1)

    count = [0]
    pending = []

    def xfer(src, dst, to):
        n = count[0]
        count[0] += 1
        return pltpu.make_async_remote_copy(
            src_ref=src, dst_ref=dst, send_sem=send.at[n], recv_sem=recv.at[n],
            device_id=to, device_id_type=pl.DeviceIdType.MESH,
        )

    def go(src, dst, to):
        copy = xfer(src, dst, to)
        copy.start()
        pending.append(copy)
        return copy

    def signal(to):
        pl.semaphore_signal(barrier, 1, device_id=to, device_id_type=pl.DeviceIdType.MESH)

    barrier = pltpu.get_barrier_semaphore()
    near = [partner] + xs + ys + [right, left]
    for p in near:
        signal(p)

    @pl.when(x != y)
    def _():
        signal(turned(0))
        signal(turned(1))

    own_rows = pl.ds(pl.multiple_of(z * RB, RU), RB)
    fcol = pl.ds(pl.multiple_of(y * FB, FB), FB)
    mine = pl.ds(pl.multiple_of(x * FB, FB), FB)
    half = [pl.ds(pl.multiple_of(k * RB, RU), RB) for k in (c, o)]
    getst = pltpu.make_async_copy(start, ST, local.at[2])
    getst.start()
    getgn = pltpu.make_async_copy(gain, GN, local.at[3])
    getgn.start()
    rmine = pltpu.make_async_copy(res.at[:, half[0]], R.at[pl.ds(c * HALF, HALF)], local.at[1])
    rmine.start()
    keep = pltpu.make_async_copy(ctx.at[half[0]], C.at[c, own_rows, mine], local.at[0])

    @pl.when(x == y)
    def _():
        keep.start()

    getst.wait()
    st = ST[...].T
    W[0] = st
    VT[0, c, :, mine] = st.astype(BF16)

    @pl.when(x != y)
    def _():
        pl.semaphore_wait(barrier, len(near) + 2)

    @pl.when(x == y)
    def _():
        pl.semaphore_wait(barrier, len(near))

    same = xfer(ctx.at[half[0]], C.at[c, own_rows, mine], turned(c))

    @pl.when(x != y)
    def _():
        same.start()

    other = go(ctx.at[half[1]], C.at[c, own_rows, mine], turned(o))

    def gather_vector(slot):
        out = [go(VT.at[slot, c, :, mine], VT.at[slot, c, :, mine], p) for p in xs]
        back = [go(VT.at[slot, c, :, mine], VT.at[slot, c, :, mine], partner)]
        return out, back

    def forward_vector(slot, out, back):
        for k in (1, 3, 2):
            out[k - 1].wait_recv()
            blk = pl.ds(pl.multiple_of(((x + NX - k) % NX) * FB, FB), FB)
            back.append(go(VT.at[slot, c, :, blk], VT.at[slot, c, :, blk], partner))

    vout, vback = gather_vector(0)
    rswap = go(res.at[:, half[1]], R.at[pl.ds(c * HALF, HALF)], partner)

    @pl.when(x != y)
    def _():
        same.wait()

    @pl.when(x == y)
    def _():
        keep.wait()

    other.wait_recv()

    def third(zz):
        return pl.ds(pl.multiple_of(zz * RB, RU), RU)

    def rest(zz):
        return pl.ds(pl.multiple_of(zz * RB + RU, RU), 2 * RU)

    def rest_of(zz, h):
        return pl.ds(pl.multiple_of(zz * RB + RU + h * RU, RU), RU)

    def send_third(h, zz, to):
        return go(C.at[h, third(zz)], C.at[h, third(zz)], to)

    def send_rest(zz, to):
        return go(C.at[:, rest(zz), fcol], C.at[:, rest(zz), fcol], to)

    def send_rest_half(h, zz, to):
        return go(C.at[h, rest(zz), fcol], C.at[h, rest(zz), fcol], to)

    def ycopies(zz, direct=False):
        if direct:
            last.extend([send_rest(zz, ys[1]), send_rest(zz, ys[0]), send_rest(zz, ys[2])])
            return []
        return [(zz, send_rest(zz, ys[0]), send_rest(zz, ys[2]))]

    last = []

    def yforward(item):
        zz, up, down = item
        below = pl.ds(pl.multiple_of(((y + NX - 1) % NX) * FB, FB), FB)
        above = pl.ds(pl.multiple_of(((y + 1) % NX) * FB, FB), FB)
        up.wait_recv()
        last.append(go(C.at[:, rest_of(zz, 0), below], C.at[:, rest_of(zz, 0), below], ys[0]))
        down.wait_recv()
        last.append(go(C.at[:, rest_of(zz, 1), above], C.at[:, rest_of(zz, 1), above], ys[2]))

    first = [dev(dy=a, dz=b) for b in (1, 0) for a in (2, 1, 3, 0) if a or b]
    second = [dev(dz=(HALF + k) % NZ) for k in sorted(range(0, NZ, 2), key=lambda v: min(v, NZ - v)) if (HALF + k) % NZ]

    def fan(buf, call, peers):
        return [go(buf.at[call, 0], buf.at[call, k + 1], p) for k, p in enumerate(peers)]

    def add_up(buf, call, copies):
        total = buf[call, 0]
        for k, copy in reversed(list(enumerate(copies))):
            copy.wait_recv()
            total = total + buf[call, k + 1]
        return total

    def fan_first(call, a1, a2):
        for j in range(nrow):
            P1[call, 0, j:j + 1, :] = a1[:, j * LB:(j + 1) * LB]
            P1[call, 0, nrow + j:nrow + j + 1, :] = a2[:, j * LB:(j + 1) * LB]
        return fan(P1, call, first)

    def fan_second(call, copies):
        P2[call, 0] = add_up(P1, call, copies)
        return fan(P2, call, second)

    def finish(call, copies):
        v = add_up(P2, call, copies)
        return (jnp.concatenate([v[j:j + 1] for j in range(nrow)], axis=1),
                jnp.concatenate([v[nrow + j:nrow + j + 1] for j in range(nrow)], axis=1))

    ar, al = send_rest(z, right), send_rest(z, left)
    y1 = [go(C.at[:, third(z), fcol], C.at[:, third(z), fcol], p) for p in ys]
    queue = [[], ycopies(z)]
    for copy in y1:
        copy.wait_recv()
    br, bl = [None, None], [None, None]
    for h in (0, 1):
        br[h], bl[h] = send_third(h, z, right), send_third(h, z, left)

    getgn.wait()
    gsq = GN[...] * GN[...]
    g2 = jnp.broadcast_to(gsq, (DB, DB)).T[:, 0:1]

    for s in range(1, HALF + 2):
        if s <= HALF:
            zr, zl = (z + NZ - s) % NZ, (z + s) % NZ
            ar.wait_recv()
            if s < HALF - 1:
                ar = send_rest(zr, right)
            elif s < HALF:
                ar = send_rest_half(0, zr, right)
            al.wait_recv()
            if s < HALF - 1:
                al = send_rest(zl, left)
            elif s < HALF:
                al = send_rest_half(1, zl, left)
            now = ycopies(zr, s >= HALF - 1)
            if s < HALF:
                now = now + ycopies(zl, s >= HALF - 1)
            queue.append(now)
        if s == HALF:
            for item in queue.pop(0):
                yforward(item)
            sums0 = fan_second(0, sums0)
        b = s - 1
        if b:
            br_at, bl_at = (z + NZ - b) % NZ, (z + b) % NZ
            for h in (0, 1):
                if b < HALF or h == 0:
                    br[h].wait_recv()
                if b < HALF - 1 or (b < HALF and h == 0):
                    br[h] = send_third(h, br_at, right)
                if b < HALF or h == 1:
                    bl[h].wait_recv()
                if b < HALF - 1 or (b < HALF and h == 1):
                    bl[h] = send_third(h, bl_at, left)
        if s < HALF:
            for item in queue.pop(0):
                yforward(item)
        if s == 3:
            forward_vector(0, vout, vback)
        if s == 4:
            rmine.wait()
            rswap.wait_recv()
            rt = R[...].reshape(NT, DB).astype(F32).T
            UT[...] = rt
            sq = rt * rt
            sums0 = fan_first(0, jnp.sum(sq, axis=0, keepdims=True), jnp.sum(sq * g2, axis=0, keepdims=True))
    for items in queue:
        for item in items:
            yforward(item)
    for copy in vback + last:
        copy.wait_recv()

    MB = NT // 2
    pairs = [(a, b) for b in range(3) for a in range(b + 1)]
    zeros = jnp.zeros((8, LB), F32)

    def gram_rows(b):
        for n, (p, q) in enumerate(pairs):
            if q == b:
                prod = jnp.sum(W[p] * W[q], axis=0, keepdims=True)
                GC[0, n:n + 1, :] = functools.reduce(
                    lambda m, v: m + v, [prod[:, j * LB:(j + 1) * LB] for j in range(FB // LB)])

    GC[0] = zeros
    for step in range(ITERS):
        def rows(m, carry, step=step):
            r = pl.ds(pl.multiple_of(m * MB, LB), MB)
            acc = lax.dot_general(C[0, r, :], VT[step, 0], (((1,), (1,)), ((), ())), preferred_element_type=F32)
            acc += lax.dot_general(C[1, r, :], VT[step, 1], (((1,), (1,)), ((), ())), preferred_element_type=F32)
            CT[:, r] = acc.T
            return carry

        if step == 0:
            lax.fori_loop(0, 2, rows, 0)
        uc = UT[...] * CT[...]
        sums = fan_first(1 + step, jnp.sum(uc, axis=0, keepdims=True), jnp.sum(uc * g2, axis=0, keepdims=True))
        if step == 0:
            s1, s2 = finish(0, sums0)
            ms = s1 / D + 1e-06
            TS[0:1, :] = 1.0 / ms
            TS[1:2, :] = 1.0 / jnp.sqrt(ms)
            TS[2:3, :] = s2 / ms
        sums = fan_second(1 + step, sums)
        gram_rows(step)
        a1, a2 = finish(1 + step, sums)
        ims, irms = TS[0:1, :], TS[1:2, :]
        along = a1 * irms / D
        back = a2 * irms / D - along * (TS[2:3, :] / D)
        ER[...] = ((g2 * (CT[...] - UT[...] * (irms * along)) - UT[...] * (irms * back)) * ims).astype(BF16)

        swaps, outs = {}, {}

        def swap(k):
            col = pl.ds(pl.multiple_of(((x + k) % NX) * FB, FB), FB)
            WS[step, :, col] = jnp.dot(ER[...], C[o, :, col], preferred_element_type=F32).astype(BF16)
            swaps[k] = go(WS.at[step, :, col], XR.at[step, :, col], partner)
            TB[k] = jnp.dot(ER[...], C[c, :, col], preferred_element_type=F32)

        def out(k):
            col = pl.ds(pl.multiple_of(((x + k) % NX) * FB, FB), FB)
            swaps[k].wait_recv()
            total = TB[k] + XR[step, :, col].astype(F32)
            if k:
                RR[step, 3 + k] = total.astype(BF16)
                outs[k] = go(RR.at[step, 3 + k], RR.at[step, k], xs[k - 1])
            return total

        order = (2, 1, 3, 0)
        swap(order[0])
        for n in (1, 2, 3):
            swap(order[n])
            out(order[n - 1])
        total = out(0)
        for k in (1, 3, 2):
            outs[k].wait_recv()
            total = total + RR[step, k].astype(F32)
        total = total * SCALE
        W[step + 1] = total
        if step + 1 < ITERS:
            VT[step + 1, c, :, mine] = total.astype(BF16)
            vout, vback = gather_vector(step + 1)

            def block(core, k, slot=step + 1):
                blk = pl.ds(pl.multiple_of(((x + NX - k) % NX) * FB, FB), FB)
                return lax.dot_general(
                    C[core, :, blk], VT[slot, core, :, blk], (((1,), (1,)), ((), ())), preferred_element_type=F32)

            def arrived(k, slot=step + 1):
                vout[k - 1].wait_recv()
                blk = pl.ds(pl.multiple_of(((x + NX - k) % NX) * FB, FB), FB)
                vback.append(go(VT.at[slot, c, :, blk], VT.at[slot, c, :, blk], partner))

            AC[...] = block(c, 0)
            vback[0].wait_recv()
            AC[...] += block(o, 0)
            arrived(1)
            AC[...] += block(c, 1)
            arrived(3)
            AC[...] += block(c, 3)
            vback[1].wait_recv()
            AC[...] += block(o, 1)
            vback[2].wait_recv()
            AC[...] += block(o, 3)
            arrived(2)
            AC[...] += block(c, 2)
            vback[3].wait_recv()
            CT[...] = (AC[...] + block(o, 2)).T

    gram_rows(2)
    copy = go(GC.at[0], GC.at[1], partner)
    copy.wait_recv()
    xy = x * NX + y
    GX[xy] = GC[0] + GC[1]
    copies = [go(GX.at[xy], GX.at[xy], dev(dx=a, dy=b)) for a in (2, 1, 3, 0) for b in (2, 1, 3, 0) if a or b]
    for copy in copies:
        copy.wait_recv()
    v = functools.reduce(lambda m, w: m + w, [GX[k] for k in range(NX * NX)])
    v = jnp.sum(v, axis=1, keepdims=True)
    lane = lax.broadcasted_iota(jnp.int32, (8, LB), 1)
    GZ[z] = jnp.sum(jnp.where(lane == lax.broadcasted_iota(jnp.int32, (8, LB), 0), v, 0.0), axis=0, keepdims=True)
    far = sorted(range(1, NZ), key=lambda k: -min(k, NZ - k))
    copies = [go(GZ.at[z], GZ.at[z], dev(dz=k)) for k in far]
    for copy in copies:
        copy.wait_recv()
    v = functools.reduce(lambda m, w: m + w, [GZ[k] for k in range(NZ)])
    g = [[None] * 3 for _ in range(3)]
    for n, (a, b) in enumerate(pairs):
        g[a][b] = g[b][a] = jnp.sum(jnp.where(lane[0:1] == n, v, 0.0), axis=1, keepdims=True)
    qs, alphas, betas = lanczos_coefs(g, float(CTX * D))
    for n, q in enumerate(qs):
        basis[n] = sum(q[k] * W[k] for k in range(n + 1)).T
    for n, value in enumerate(alphas + betas):
        ab[n:n + 1, :] = jnp.broadcast_to(value, (1, LB))
    ab[4:8, :] = jnp.zeros((4, LB), F32)
    for copy in pending:
        copy.wait_send()


def body(cfg, context, residual, gain, start):
    NZ, RU, FB, DB, D, CTX = cfg
    NT, RB = NZ * 3 * RU, 3 * RU
    vmem = pl.BlockSpec(memory_space=pltpu.VMEM)
    flops = 8 * NT * CTX * DB
    basis, ab = pl.pallas_call(
        functools.partial(kernel, cfg),
        out_shape=(jax.ShapeDtypeStruct((3, FB, DB), F32), jax.ShapeDtypeStruct((8, LB), F32)),
        in_specs=[pl.BlockSpec(memory_space=pltpu.HBM)] * 4,
        out_specs=(vmem, vmem),
        scratch_shapes=[
            pltpu.VMEM((2, NT, NX * FB), BF16),
            pltpu.VMEM((NZ, RB, DB), BF16),
            pltpu.VMEM((FB, DB), F32),
            pltpu.VMEM((1, DB), F32),
            pltpu.VMEM((ITERS, 2, DB, NX * FB), BF16),
            pltpu.VMEM((DB, NT), F32),
            pltpu.VMEM((DB, NT), F32),
            pltpu.VMEM((NT, DB), F32),
            pltpu.VMEM((8, NT), F32),
            pltpu.VMEM((DB, NT), BF16),
            pltpu.VMEM((ITERS, DB, NX * FB), BF16),
            pltpu.VMEM((ITERS, DB, NX * FB), BF16),
            pltpu.VMEM((4, DB, FB), F32),
            pltpu.VMEM((ITERS, 7, DB, FB), BF16),
            pltpu.VMEM((3, DB, FB), F32),
            pltpu.VMEM((ITERS + 1, 8, 2 * (NT // LB), LB), F32),
            pltpu.VMEM((ITERS + 1, NZ // 2, 2 * (NT // LB), LB), F32),
            pltpu.VMEM((2, 8, LB), F32),
            pltpu.VMEM((NX * NX, 8, LB), F32),
            pltpu.VMEM((NZ, 1, LB), F32),
            pltpu.SemaphoreType.DMA((320,)),
            pltpu.SemaphoreType.DMA((320,)),
            pltpu.SemaphoreType.DMA((4,)),
        ],
        compiler_params=pltpu.CompilerParams(collective_id=0, has_side_effects=True, vmem_limit_bytes=40 * 2 ** 20),
        cost_estimate=pl.CostEstimate(flops=flops, bytes_accessed=2 ** 21, transcendentals=0),
    )(context, residual.reshape(NZ // 2, 2 * RB, DB), gain.reshape(1, DB), start)
    return basis, ab[0:2, 0], ab[2:4, 0]


def solution(mesh):
    cfg = (16, 16, 512, 128, 8192, 4096)
    in_specs = (P("dp", "tensor"), P("tensor", "dp"), P("dp"), P("tensor", "dp"))
    out_specs = (P(None, "tensor", "dp"), P(), P())
    return jax.shard_map(
        functools.partial(body, cfg), mesh=mesh, in_specs=in_specs, out_specs=out_specs, check_vma=False)
```

```python
import functools

import jax
import jax.numpy as jnp
from jax import lax
from jax.experimental import pallas as pl
from jax.experimental.pallas import tpu as pltpu
from jax.sharding import PartitionSpec as P

ITERS = 2
SCALE = 2.0 ** -20
NX = 4
LB = 128
F32, BF16 = jnp.float32, jnp.bfloat16


def lanczos_coefs(g, total):
    g = [[g[i][j] / total for j in range(3)] for i in range(3)]

    def inner(a, b):
        return sum(a[i] * b[j] * g[i][j] for i in range(3) for j in range(3))

    def axpy(a, b, s):
        return [b[i] - s * a[i] for i in range(3)]

    zero = jnp.zeros_like(g[0][0])
    inv = 1.0 / jnp.sqrt(g[0][0] + 1e-06)
    q0 = [inv, zero, zero]
    w1 = [zero, inv / SCALE, zero]
    h00 = inner(q0, w1)
    r1 = axpy(q0, w1, h00)
    b0 = jnp.sqrt(jnp.maximum(inner(r1, r1), 0.0) + 1e-06)
    q1 = [v / b0 for v in r1]
    gw1 = [zero, zero, inv / SCALE / SCALE]
    w2 = [v / b0 for v in axpy(w1, gw1, h00)]
    h01 = inner(q0, w2)
    h11 = inner(q1, w2)
    r2 = axpy(q1, axpy(q0, w2, h01), h11)
    b1 = jnp.sqrt(jnp.maximum(inner(r2, r2), 0.0) + 1e-06)
    q2 = [v / b1 for v in r2]
    return (q0, q1, q2), (h00, h11), (b0, b1)


def kernel(cfg, ctx, res, gain, start, basis, ab, C, R, ST, GN, VT, UT, CT, TS, ER, WS, XR, TB, RR, W, P1, P2, GC, GX, GZ, send, recv, local):
    NZ, RU, FB, DB, D, CTX = cfg
    NT = NZ * 3 * RU
    RB = 3 * RU
    HALF = NZ // 2
    nrow = NT // LB
    i = lax.axis_index("dp")
    t = lax.axis_index("tensor")
    y, z = i // NZ, i % NZ
    x, c = t // 2, t % 2
    o = 1 - c

    def dev(dx=0, dy=0, dz=0, core=None):
        return {
            "dp": ((y + dy) % NX) * NZ + (z + dz) % NZ,
            "tensor": ((x + dx) % NX) * 2 + (c if core is None else core),
        }

    def turned(core):
        return {"dp": x * NZ + z, "tensor": y * 2 + core}

    partner = dev(core=o)
    xs = [dev(dx=k) for k in (1, 2, 3)]
    ys = [dev(dy=k) for k in (1, 2, 3)]
    right, left = dev(dz=1), dev(dz=NZ - 1)

    count = [0]
    pending = []

    def xfer(src, dst, to):
        n = count[0]
        count[0] += 1
        return pltpu.make_async_remote_copy(
            src_ref=src, dst_ref=dst, send_sem=send.at[n], recv_sem=recv.at[n],
            device_id=to, device_id_type=pl.DeviceIdType.MESH,
        )

    def go(src, dst, to):
        copy = xfer(src, dst, to)
        copy.start()
        pending.append(copy)
        return copy

    def drain(keep):
        for copy in pending[:len(pending) - keep]:
            copy.wait_send()
        del pending[:len(pending) - keep]

    def signal(to):
        pl.semaphore_signal(barrier, 1, device_id=to, device_id_type=pl.DeviceIdType.MESH)

    barrier = pltpu.get_barrier_semaphore()
    near = [partner] + xs + ys + [right, left]
    for p in near:
        signal(p)

    @pl.when(x != y)
    def _():
        signal(turned(0))
        signal(turned(1))

    own_rows = pl.ds(pl.multiple_of(z * RB, RU), RB)
    fcol = pl.ds(pl.multiple_of(y * FB, FB), FB)
    mine = pl.ds(pl.multiple_of(x * FB, FB), FB)
    half = [pl.ds(pl.multiple_of(k * RB, RU), RB) for k in (c, o)]
    getst = pltpu.make_async_copy(start, ST, local.at[2])
    getst.start()
    getgn = pltpu.make_async_copy(gain, GN, local.at[3])
    getgn.start()
    rmine = pltpu.make_async_copy(res.at[:, half[0]], R.at[pl.ds(c * HALF, HALF)], local.at[1])
    rmine.start()
    keep = pltpu.make_async_copy(ctx.at[half[0]], C.at[c, own_rows, mine], local.at[0])

    @pl.when(x == y)
    def _():
        keep.start()

    getst.wait()
    st = ST[...].T
    W[0] = st
    VT[0, c, :, mine] = st.astype(BF16)

    @pl.when(x != y)
    def _():
        pl.semaphore_wait(barrier, len(near) + 2)

    @pl.when(x == y)
    def _():
        pl.semaphore_wait(barrier, len(near))

    same = xfer(ctx.at[half[0]], C.at[c, own_rows, mine], turned(c))

    @pl.when(x != y)
    def _():
        same.start()

    other = go(ctx.at[half[1]], C.at[c, own_rows, mine], turned(o))

    def gather_vector(slot):
        out = [go(VT.at[slot, c, :, mine], VT.at[slot, c, :, mine], p) for p in xs]
        back = [go(VT.at[slot, c, :, mine], VT.at[slot, c, :, mine], partner)]
        return out, back

    def forward_vector(slot, out, back):
        for k in (1, 3, 2):
            out[k - 1].wait_recv()
            blk = pl.ds(pl.multiple_of(((x + NX - k) % NX) * FB, FB), FB)
            back.append(go(VT.at[slot, c, :, blk], VT.at[slot, c, :, blk], partner))

    vout, vback = gather_vector(0)
    rswap = go(res.at[:, half[1]], R.at[pl.ds(c * HALF, HALF)], partner)

    @pl.when(x != y)
    def _():
        same.wait()

    @pl.when(x == y)
    def _():
        keep.wait()

    other.wait_recv()

    def third(zz):
        return pl.ds(pl.multiple_of(zz * RB, RU), RU)

    def rest(zz):
        return pl.ds(pl.multiple_of(zz * RB + RU, RU), 2 * RU)

    def rest_of(zz, h):
        return pl.ds(pl.multiple_of(zz * RB + RU + h * RU, RU), RU)

    def send_third(h, zz, to):
        return go(C.at[h, third(zz)], C.at[h, third(zz)], to)

    def send_rest(zz, to):
        return go(C.at[:, rest(zz), fcol], C.at[:, rest(zz), fcol], to)

    def send_rest_half(h, zz, to):
        return go(C.at[h, rest(zz), fcol], C.at[h, rest(zz), fcol], to)

    def ycopies(zz):
        return zz, send_rest(zz, ys[0]), send_rest(zz, ys[2])

    last = []

    def yforward(item):
        zz, up, down = item
        below = pl.ds(pl.multiple_of(((y + NX - 1) % NX) * FB, FB), FB)
        above = pl.ds(pl.multiple_of(((y + 1) % NX) * FB, FB), FB)
        up.wait_recv()
        last.append(go(C.at[:, rest_of(zz, 0), below], C.at[:, rest_of(zz, 0), below], ys[0]))
        down.wait_recv()
        last.append(go(C.at[:, rest_of(zz, 1), above], C.at[:, rest_of(zz, 1), above], ys[2]))

    first = [dev(dy=a, dz=b) for b in (1, 0) for a in (2, 1, 3, 0) if a or b]
    second = [dev(dz=(HALF + k) % NZ) for k in sorted(range(0, NZ, 2), key=lambda v: min(v, NZ - v)) if (HALF + k) % NZ]

    def fan(buf, call, peers):
        return [go(buf.at[call, 0], buf.at[call, k + 1], p) for k, p in enumerate(peers)]

    def add_up(buf, call, copies):
        total = buf[call, 0]
        for k, copy in reversed(list(enumerate(copies))):
            copy.wait_recv()
            total = total + buf[call, k + 1]
        return total

    def fan_first(call, a1, a2):
        for j in range(nrow):
            P1[call, 0, j:j + 1, :] = a1[:, j * LB:(j + 1) * LB]
            P1[call, 0, nrow + j:nrow + j + 1, :] = a2[:, j * LB:(j + 1) * LB]
        return fan(P1, call, first)

    def fan_second(call, copies):
        P2[call, 0] = add_up(P1, call, copies)
        return fan(P2, call, second)

    def finish(call, copies):
        v = add_up(P2, call, copies)
        return (jnp.concatenate([v[j:j + 1] for j in range(nrow)], axis=1),
                jnp.concatenate([v[nrow + j:nrow + j + 1] for j in range(nrow)], axis=1))

    ar, al = [None, None], [None, None]
    for h in (0, 1):
        ar[h], al[h] = send_rest_half(h, z, right), send_rest_half(h, z, left)
    y1 = [go(C.at[:, third(z), fcol], C.at[:, third(z), fcol], p) for p in ys]
    queue = [[], [ycopies(z)]]
    for copy in y1:
        copy.wait_recv()
    br, bl = [None, None], [None, None]
    for h in (0, 1):
        br[h], bl[h] = send_third(h, z, right), send_third(h, z, left)

    getgn.wait()
    gsq = GN[...] * GN[...]
    g2 = jnp.broadcast_to(gsq, (DB, DB)).T[:, 0:1]

    for s in range(1, HALF + 1):
        zr, zl = (z + NZ - s) % NZ, (z + s) % NZ
        end = s == HALF
        for h in (0, 1):
            if not end or h == 0:
                ar[h].wait_recv()
            if s < HALF - 1 or (not end and h == 0):
                ar[h] = send_rest_half(h, zr, right)
            if not end or h == 1:
                al[h].wait_recv()
            if s < HALF - 1 or (not end and h == 1):
                al[h] = send_rest_half(h, zl, left)
        now = [ycopies(zr)] if end else [ycopies(zr), ycopies(zl)]
        if end:
            sums0 = fan_second(0, sums0)
        for h in (0, 1):
            if not end or h == 0:
                br[h].wait_recv()
            if s < HALF - 1 or (not end and h == 0):
                br[h] = send_third(h, zr, right)
            if not end or h == 1:
                bl[h].wait_recv()
            if s < HALF - 1 or (not end and h == 1):
                bl[h] = send_third(h, zl, left)
        queue.append(now)
        for item in queue.pop(0):
            yforward(item)
        if s == 3:
            forward_vector(0, vout, vback)
        if s == 2:
            rmine.wait()
            rswap.wait_recv()
            rt = R[...].reshape(NT, DB).astype(F32).T
            UT[...] = rt
            sq = rt * rt
            sums0 = fan_first(0, jnp.sum(sq, axis=0, keepdims=True), jnp.sum(sq * g2, axis=0, keepdims=True))
    for items in queue:
        for item in items:
            yforward(item)
    for copy in vback + last:
        copy.wait_recv()

    MB = NT // 2
    pairs = [(a, b) for b in range(3) for a in range(b + 1)]
    zeros = jnp.zeros((8, LB), F32)

    def gram_rows(b):
        for n, (p, q) in enumerate(pairs):
            if q == b:
                prod = jnp.sum(W[p] * W[q], axis=0, keepdims=True)
                GC[0, n:n + 1, :] = functools.reduce(
                    lambda m, v: m + v, [prod[:, j * LB:(j + 1) * LB] for j in range(FB // LB)])

    GC[0] = zeros
    for step in range(ITERS):
        def rows(m, carry, step=step):
            r = pl.ds(pl.multiple_of(m * MB, LB), MB)
            acc = lax.dot_general(C[0, r, :], VT[step, 0], (((1,), (1,)), ((), ())), preferred_element_type=F32)
            acc += lax.dot_general(C[1, r, :], VT[step, 1], (((1,), (1,)), ((), ())), preferred_element_type=F32)
            CT[:, r] = acc.T
            return carry

        lax.fori_loop(0, 2, rows, 0)
        uc = UT[...] * CT[...]
        sums = fan_first(1 + step, jnp.sum(uc, axis=0, keepdims=True), jnp.sum(uc * g2, axis=0, keepdims=True))
        drain(len(sums))
        if step == 0:
            s1, s2 = finish(0, sums0)
            ms = s1 / D + 1e-06
            TS[0:1, :] = 1.0 / ms
            TS[1:2, :] = 1.0 / jnp.sqrt(ms)
            TS[2:3, :] = s2 / ms
        sums = fan_second(1 + step, sums)
        gram_rows(step)
        a1, a2 = finish(1 + step, sums)
        ims, irms = TS[0:1, :], TS[1:2, :]
        along = a1 * irms / D
        back = a2 * irms / D - along * (TS[2:3, :] / D)
        ER[...] = ((g2 * (CT[...] - UT[...] * (irms * along)) - UT[...] * (irms * back)) * ims).astype(BF16)

        swaps, outs = {}, {}

        def swap(k):
            col = pl.ds(pl.multiple_of(((x + k) % NX) * FB, FB), FB)
            WS[step, :, col] = jnp.dot(ER[...], C[o, :, col], preferred_element_type=F32).astype(BF16)
            swaps[k] = go(WS.at[step, :, col], XR.at[step, :, col], partner)
            TB[k] = jnp.dot(ER[...], C[c, :, col], preferred_element_type=F32)

        def out(k):
            col = pl.ds(pl.multiple_of(((x + k) % NX) * FB, FB), FB)
            swaps[k].wait_recv()
            total = TB[k] + XR[step, :, col].astype(F32)
            if k:
                RR[step, 3 + k] = total.astype(BF16)
                outs[k] = go(RR.at[step, 3 + k], RR.at[step, k], xs[k - 1])
            return total

        order = (2, 1, 3, 0)
        swap(order[0])
        for n in (1, 2, 3):
            swap(order[n])
            out(order[n - 1])
        total = out(0)
        for k in (1, 3, 2):
            outs[k].wait_recv()
            total = total + RR[step, k].astype(F32)
        total = total * SCALE
        W[step + 1] = total
        if step + 1 < ITERS:
            VT[step + 1, c, :, mine] = total.astype(BF16)
            vout, vback = gather_vector(step + 1)
            forward_vector(step + 1, vout, vback)
            for copy in vback:
                copy.wait_recv()

    gram_rows(2)
    copy = go(GC.at[0], GC.at[1], partner)
    copy.wait_recv()
    xy = x * NX + y
    GX[xy] = GC[0] + GC[1]
    copies = [go(GX.at[xy], GX.at[xy], dev(dx=a, dy=b)) for a in (2, 1, 3, 0) for b in (2, 1, 3, 0) if a or b]
    for copy in copies:
        copy.wait_recv()
    v = functools.reduce(lambda m, w: m + w, [GX[k] for k in range(NX * NX)])
    v = jnp.sum(v, axis=1, keepdims=True)
    lane = lax.broadcasted_iota(jnp.int32, (8, LB), 1)
    GZ[z] = jnp.sum(jnp.where(lane == lax.broadcasted_iota(jnp.int32, (8, LB), 0), v, 0.0), axis=0, keepdims=True)
    far = sorted(range(1, NZ), key=lambda k: -min(k, NZ - k))
    copies = [go(GZ.at[z], GZ.at[z], dev(dz=k)) for k in far]
    drain(len(far))
    for copy in copies:
        copy.wait_recv()
    v = functools.reduce(lambda m, w: m + w, [GZ[k] for k in range(NZ)])
    g = [[None] * 3 for _ in range(3)]
    for n, (a, b) in enumerate(pairs):
        g[a][b] = g[b][a] = jnp.sum(jnp.where(lane[0:1] == n, v, 0.0), axis=1, keepdims=True)
    qs, alphas, betas = lanczos_coefs(g, float(CTX * D))
    for n, q in enumerate(qs):
        basis[n] = sum(q[k] * W[k] for k in range(n + 1)).T
    for n, value in enumerate(alphas + betas):
        ab[n:n + 1, :] = jnp.broadcast_to(value, (1, LB))
    ab[4:8, :] = jnp.zeros((4, LB), F32)
    drain(0)


def body(cfg, context, residual, gain, start):
    NZ, RU, FB, DB, D, CTX = cfg
    NT, RB = NZ * 3 * RU, 3 * RU
    vmem = pl.BlockSpec(memory_space=pltpu.VMEM)
    flops = 8 * NT * CTX * DB
    basis, ab = pl.pallas_call(
        functools.partial(kernel, cfg),
        out_shape=(jax.ShapeDtypeStruct((3, FB, DB), F32), jax.ShapeDtypeStruct((8, LB), F32)),
        in_specs=[pl.BlockSpec(memory_space=pltpu.HBM)] * 4,
        out_specs=(vmem, vmem),
        scratch_shapes=[
            pltpu.VMEM((2, NT, NX * FB), BF16),
            pltpu.VMEM((NZ, RB, DB), BF16),
            pltpu.VMEM((FB, DB), F32),
            pltpu.VMEM((1, DB), F32),
            pltpu.VMEM((ITERS, 2, DB, NX * FB), BF16),
            pltpu.VMEM((DB, NT), F32),
            pltpu.VMEM((DB, NT), F32),
            pltpu.VMEM((8, NT), F32),
            pltpu.VMEM((DB, NT), BF16),
            pltpu.VMEM((ITERS, DB, NX * FB), BF16),
            pltpu.VMEM((ITERS, DB, NX * FB), BF16),
            pltpu.VMEM((4, DB, FB), F32),
            pltpu.VMEM((ITERS, 7, DB, FB), BF16),
            pltpu.VMEM((3, DB, FB), F32),
            pltpu.VMEM((ITERS + 1, 8, 2 * (NT // LB), LB), F32),
            pltpu.VMEM((ITERS + 1, NZ // 2, 2 * (NT // LB), LB), F32),
            pltpu.VMEM((2, 8, LB), F32),
            pltpu.VMEM((NX * NX, 8, LB), F32),
            pltpu.VMEM((NZ, 1, LB), F32),
            pltpu.SemaphoreType.DMA((320,)),
            pltpu.SemaphoreType.DMA((320,)),
            pltpu.SemaphoreType.DMA((4,)),
        ],
        compiler_params=pltpu.CompilerParams(collective_id=0, has_side_effects=True, vmem_limit_bytes=40 * 2 ** 20),
        cost_estimate=pl.CostEstimate(flops=flops, bytes_accessed=2 ** 21, transcendentals=0),
    )(context, residual.reshape(NZ // 2, 2 * RB, DB), gain.reshape(1, DB), start)
    return basis, ab[0:2, 0], ab[2:4, 0]


def solution(mesh):
    cfg = (16, 16, 512, 128, 8192, 4096)
    in_specs = (P("dp", "tensor"), P("tensor", "dp"), P("dp"), P("tensor", "dp"))
    out_specs = (P(None, "tensor", "dp"), P(), P())
    return jax.shard_map(
        functools.partial(body, cfg), mesh=mesh, in_specs=in_specs, out_specs=out_specs, check_vma=False)
```

```python
import functools

import jax
import jax.numpy as jnp
from jax import lax
from jax.experimental import pallas as pl
from jax.experimental.pallas import tpu as pltpu
from jax.sharding import PartitionSpec as P

ITERS = 2
SCALE = 2.0 ** -20
NX = 4
LB = 128
F32, BF16 = jnp.float32, jnp.bfloat16


def lanczos_coefs(g, total):
    g = [[g[i][j] / total for j in range(3)] for i in range(3)]

    def inner(a, b):
        return sum(a[i] * b[j] * g[i][j] for i in range(3) for j in range(3))

    def axpy(a, b, s):
        return [b[i] - s * a[i] for i in range(3)]

    zero = jnp.zeros_like(g[0][0])
    inv = 1.0 / jnp.sqrt(g[0][0] + 1e-06)
    q0 = [inv, zero, zero]
    w1 = [zero, inv / SCALE, zero]
    h00 = inner(q0, w1)
    r1 = axpy(q0, w1, h00)
    b0 = jnp.sqrt(jnp.maximum(inner(r1, r1), 0.0) + 1e-06)
    q1 = [v / b0 for v in r1]
    gw1 = [zero, zero, inv / SCALE / SCALE]
    w2 = [v / b0 for v in axpy(w1, gw1, h00)]
    h01 = inner(q0, w2)
    h11 = inner(q1, w2)
    r2 = axpy(q1, axpy(q0, w2, h01), h11)
    b1 = jnp.sqrt(jnp.maximum(inner(r2, r2), 0.0) + 1e-06)
    q2 = [v / b1 for v in r2]
    return (q0, q1, q2), (h00, h11), (b0, b1)


def kernel(cfg, ctx, res, gain, start, basis, ab, C, R, ST, GN, VT, UT, CT, TS, ER, WS, XR, TB, RR, W, P1, P2, GC, GX, GZ, send, recv, local):
    NZ, RU, FB, DB, D, CTX = cfg
    NT = NZ * 3 * RU
    RB = 3 * RU
    HALF = NZ // 2
    nrow = NT // LB
    i = lax.axis_index("dp")
    t = lax.axis_index("tensor")
    y, z = i // NZ, i % NZ
    x, c = t // 2, t % 2
    o = 1 - c

    def dev(dx=0, dy=0, dz=0, core=None):
        return {
            "dp": ((y + dy) % NX) * NZ + (z + dz) % NZ,
            "tensor": ((x + dx) % NX) * 2 + (c if core is None else core),
        }

    def turned(core):
        return {"dp": x * NZ + z, "tensor": y * 2 + core}

    partner = dev(core=o)
    xs = [dev(dx=k) for k in (1, 2, 3)]
    ys = [dev(dy=k) for k in (1, 2, 3)]
    right, left = dev(dz=1), dev(dz=NZ - 1)

    count = [0]
    pending = []

    def xfer(src, dst, to):
        n = count[0]
        count[0] += 1
        return pltpu.make_async_remote_copy(
            src_ref=src, dst_ref=dst, send_sem=send.at[n], recv_sem=recv.at[n],
            device_id=to, device_id_type=pl.DeviceIdType.MESH,
        )

    def go(src, dst, to):
        copy = xfer(src, dst, to)
        copy.start()
        pending.append(copy)
        return copy

    def drain(keep):
        for copy in pending[:len(pending) - keep]:
            copy.wait_send()
        del pending[:len(pending) - keep]

    def signal(to):
        pl.semaphore_signal(barrier, 1, device_id=to, device_id_type=pl.DeviceIdType.MESH)

    barrier = pltpu.get_barrier_semaphore()
    near = [partner] + xs + ys + [right, left]
    for p in near:
        signal(p)

    @pl.when(x != y)
    def _():
        signal(turned(0))
        signal(turned(1))

    own_rows = pl.ds(pl.multiple_of(z * RB, RU), RB)
    fcol = pl.ds(pl.multiple_of(y * FB, FB), FB)
    mine = pl.ds(pl.multiple_of(x * FB, FB), FB)
    half = [pl.ds(pl.multiple_of(k * RB, RU), RB) for k in (c, o)]
    getst = pltpu.make_async_copy(start, ST, local.at[2])
    getst.start()
    getgn = pltpu.make_async_copy(gain, GN, local.at[3])
    getgn.start()
    rmine = pltpu.make_async_copy(res.at[:, half[0]], R.at[pl.ds(c * HALF, HALF)], local.at[1])
    rmine.start()
    keep = pltpu.make_async_copy(ctx.at[half[0]], C.at[c, own_rows, mine], local.at[0])

    @pl.when(x == y)
    def _():
        keep.start()

    getst.wait()
    st = ST[...].T
    W[0] = st
    VT[0, c, :, mine] = st.astype(BF16)

    @pl.when(x != y)
    def _():
        pl.semaphore_wait(barrier, len(near) + 2)

    @pl.when(x == y)
    def _():
        pl.semaphore_wait(barrier, len(near))

    same = xfer(ctx.at[half[0]], C.at[c, own_rows, mine], turned(c))

    @pl.when(x != y)
    def _():
        same.start()

    other = go(ctx.at[half[1]], C.at[c, own_rows, mine], turned(o))

    def gather_vector(slot):
        out = [go(VT.at[slot, c, :, mine], VT.at[slot, c, :, mine], p) for p in xs]
        back = [go(VT.at[slot, c, :, mine], VT.at[slot, c, :, mine], partner)]
        return out, back

    def forward_vector(slot, out, back):
        for k in (1, 3, 2):
            out[k - 1].wait_recv()
            blk = pl.ds(pl.multiple_of(((x + NX - k) % NX) * FB, FB), FB)
            back.append(go(VT.at[slot, c, :, blk], VT.at[slot, c, :, blk], partner))

    vout, vback = gather_vector(0)
    rswap = go(res.at[:, half[1]], R.at[pl.ds(c * HALF, HALF)], partner)

    @pl.when(x != y)
    def _():
        same.wait()

    @pl.when(x == y)
    def _():
        keep.wait()

    other.wait_recv()

    def third(zz):
        return pl.ds(pl.multiple_of(zz * RB, RU), RU)

    def rest(zz):
        return pl.ds(pl.multiple_of(zz * RB + RU, RU), 2 * RU)

    def rest_of(zz, h):
        return pl.ds(pl.multiple_of(zz * RB + RU + h * RU, RU), RU)

    def send_third(h, zz, to):
        return go(C.at[h, third(zz)], C.at[h, third(zz)], to)

    def send_rest(zz, to):
        return go(C.at[:, rest(zz), fcol], C.at[:, rest(zz), fcol], to)

    def send_rest_half(h, zz, to):
        return go(C.at[h, rest(zz), fcol], C.at[h, rest(zz), fcol], to)

    def ycopies(zz):
        return zz, send_rest(zz, ys[0]), send_rest(zz, ys[2])

    last = []

    def yforward(item):
        zz, up, down = item
        below = pl.ds(pl.multiple_of(((y + NX - 1) % NX) * FB, FB), FB)
        above = pl.ds(pl.multiple_of(((y + 1) % NX) * FB, FB), FB)
        up.wait_recv()
        last.append(go(C.at[:, rest_of(zz, 0), below], C.at[:, rest_of(zz, 0), below], ys[0]))
        down.wait_recv()
        last.append(go(C.at[:, rest_of(zz, 1), above], C.at[:, rest_of(zz, 1), above], ys[2]))

    first = [dev(dy=a, dz=b) for b in (1, 0) for a in (2, 1, 3, 0) if a or b]
    second = [dev(dz=(HALF + k) % NZ) for k in sorted(range(0, NZ, 2), key=lambda v: min(v, NZ - v)) if (HALF + k) % NZ]

    def fan(buf, call, peers):
        return [go(buf.at[call, 0], buf.at[call, k + 1], p) for k, p in enumerate(peers)]

    def add_up(buf, call, copies):
        total = buf[call, 0]
        for k, copy in reversed(list(enumerate(copies))):
            copy.wait_recv()
            total = total + buf[call, k + 1]
        return total

    def fan_first(call, a1, a2):
        for j in range(nrow):
            P1[call, 0, j:j + 1, :] = a1[:, j * LB:(j + 1) * LB]
            P1[call, 0, nrow + j:nrow + j + 1, :] = a2[:, j * LB:(j + 1) * LB]
        return fan(P1, call, first)

    def fan_second(call, copies):
        P2[call, 0] = add_up(P1, call, copies)
        return fan(P2, call, second)

    def finish(call, copies):
        v = add_up(P2, call, copies)
        return (jnp.concatenate([v[j:j + 1] for j in range(nrow)], axis=1),
                jnp.concatenate([v[nrow + j:nrow + j + 1] for j in range(nrow)], axis=1))

    ar, al = [None, None], [None, None]
    for h in (0, 1):
        ar[h], al[h] = send_rest_half(h, z, right), send_rest_half(h, z, left)
    y1 = [go(C.at[:, third(z), fcol], C.at[:, third(z), fcol], p) for p in ys]
    queue = [[], [ycopies(z)]]
    for copy in y1:
        copy.wait_recv()
    br, bl = [None, None], [None, None]
    for h in (0, 1):
        br[h], bl[h] = send_third(h, z, right), send_third(h, z, left)

    getgn.wait()
    gsq = GN[...] * GN[...]
    g2 = jnp.broadcast_to(gsq, (DB, DB)).T[:, 0:1]

    for s in range(1, HALF + 1):
        zr, zl = (z + NZ - s) % NZ, (z + s) % NZ
        end = s == HALF
        for h in (0, 1):
            if not end or h == 0:
                ar[h].wait_recv()
            if s < HALF - 1 or (not end and h == 0):
                ar[h] = send_rest_half(h, zr, right)
            if not end or h == 1:
                al[h].wait_recv()
            if s < HALF - 1 or (not end and h == 1):
                al[h] = send_rest_half(h, zl, left)
        now = [ycopies(zr)] if end else [ycopies(zr), ycopies(zl)]
        if end:
            sums0 = fan_second(0, sums0)
        for h in (0, 1):
            if not end or h == 0:
                br[h].wait_recv()
            if s < HALF - 1 or (not end and h == 0):
                br[h] = send_third(h, zr, right)
            if not end or h == 1:
                bl[h].wait_recv()
            if s < HALF - 1 or (not end and h == 1):
                bl[h] = send_third(h, zl, left)
        queue.append(now)
        for item in queue.pop(0):
            yforward(item)
        if s == 3:
            forward_vector(0, vout, vback)
        if s == 2:
            rmine.wait()
            rswap.wait_recv()
            rt = R[...].reshape(NT, DB).astype(F32).T
            UT[...] = rt
            sq = rt * rt
            sums0 = fan_first(0, jnp.sum(sq, axis=0, keepdims=True), jnp.sum(sq * g2, axis=0, keepdims=True))
    for items in queue:
        for item in items:
            yforward(item)
    for copy in vback + last:
        copy.wait_recv()

    MB = NT // 2
    pairs = [(a, b) for b in range(3) for a in range(b + 1)]
    zeros = jnp.zeros((8, LB), F32)

    def gram_rows(b):
        for n, (p, q) in enumerate(pairs):
            if q == b:
                prod = jnp.sum(W[p] * W[q], axis=0, keepdims=True)
                GC[0, n:n + 1, :] = functools.reduce(
                    lambda m, v: m + v, [prod[:, j * LB:(j + 1) * LB] for j in range(FB // LB)])

    GC[0] = zeros
    for step in range(ITERS):
        def rows(m, carry, step=step):
            r = pl.ds(pl.multiple_of(m * MB, LB), MB)
            acc = lax.dot_general(C[0, r, :], VT[step, 0], (((1,), (1,)), ((), ())), preferred_element_type=F32)
            acc += lax.dot_general(C[1, r, :], VT[step, 1], (((1,), (1,)), ((), ())), preferred_element_type=F32)
            CT[:, r] = acc.T
            return carry

        lax.fori_loop(0, 2, rows, 0)
        uc = UT[...] * CT[...]
        sums = fan_first(1 + step, jnp.sum(uc, axis=0, keepdims=True), jnp.sum(uc * g2, axis=0, keepdims=True))
        drain(len(sums))
        if step == 0:
            s1, s2 = finish(0, sums0)
            ms = s1 / D + 1e-06
            TS[0:1, :] = 1.0 / ms
            TS[1:2, :] = 1.0 / jnp.sqrt(ms)
            TS[2:3, :] = s2 / ms
        sums = fan_second(1 + step, sums)
        gram_rows(step)
        a1, a2 = finish(1 + step, sums)
        ims, irms = TS[0:1, :], TS[1:2, :]
        along = a1 * irms / D
        back = a2 * irms / D - along * (TS[2:3, :] / D)
        ER[...] = ((g2 * (CT[...] - UT[...] * (irms * along)) - UT[...] * (irms * back)) * ims).astype(BF16)

        swaps, outs = {}, {}

        def swap(k):
            col = pl.ds(pl.multiple_of(((x + k) % NX) * FB, FB), FB)
            WS[step, :, col] = jnp.dot(ER[...], C[o, :, col], preferred_element_type=F32).astype(BF16)
            swaps[k] = go(WS.at[step, :, col], XR.at[step, :, col], partner)
            TB[k] = jnp.dot(ER[...], C[c, :, col], preferred_element_type=F32)

        def out(k):
            col = pl.ds(pl.multiple_of(((x + k) % NX) * FB, FB), FB)
            swaps[k].wait_recv()
            total = TB[k] + XR[step, :, col].astype(F32)
            if k:
                RR[step, 3 + k] = total.astype(BF16)
                outs[k] = go(RR.at[step, 3 + k], RR.at[step, k], xs[k - 1])
            return total

        order = (2, 1, 3, 0)
        swap(order[0])
        for n in (1, 2, 3):
            swap(order[n])
            out(order[n - 1])
        total = out(0)
        for k in (1, 3, 2):
            outs[k].wait_recv()
            total = total + RR[step, k].astype(F32)
        total = total * SCALE
        W[step + 1] = total
        if step + 1 < ITERS:
            VT[step + 1, c, :, mine] = total.astype(BF16)
            vout, vback = gather_vector(step + 1)
            forward_vector(step + 1, vout, vback)
            for copy in vback:
                copy.wait_recv()

    gram_rows(2)
    me = (x * NX + y) * 2 + c
    GX[me] = GC[0]
    copies = [
        go(GX.at[me], GX.at[me], dev(dx=a, dy=b, core=k))
        for a in (2, 1, 3, 0) for b in (2, 1, 3, 0) for k in ((c, o) if a or b else (o,))
    ]
    for copy in copies:
        copy.wait_recv()
    parts = [GX[k] for k in range(2 * NX * NX)]
    while len(parts) > 1:
        parts = [p + q for p, q in zip(parts[::2], parts[1::2])]
    v = parts[0]
    v = jnp.sum(v, axis=1, keepdims=True)
    lane = lax.broadcasted_iota(jnp.int32, (8, LB), 1)
    GZ[z] = jnp.sum(jnp.where(lane == lax.broadcasted_iota(jnp.int32, (8, LB), 0), v, 0.0), axis=0, keepdims=True)
    far = sorted(range(1, NZ), key=lambda k: -min(k, NZ - k))
    copies = [go(GZ.at[z], GZ.at[z], dev(dz=k)) for k in far]
    drain(len(far))
    for copy in copies:
        copy.wait_recv()
    v = functools.reduce(lambda m, w: m + w, [GZ[k] for k in range(NZ)])
    g = [[None] * 3 for _ in range(3)]
    for n, (a, b) in enumerate(pairs):
        g[a][b] = g[b][a] = jnp.sum(jnp.where(lane[0:1] == n, v, 0.0), axis=1, keepdims=True)
    qs, alphas, betas = lanczos_coefs(g, float(CTX * D))
    for n, q in enumerate(qs):
        basis[n] = sum(q[k] * W[k] for k in range(n + 1)).T
    for n, value in enumerate(alphas + betas):
        ab[n:n + 1, :] = jnp.broadcast_to(value, (1, LB))
    ab[4:8, :] = jnp.zeros((4, LB), F32)
    drain(0)


def body(cfg, context, residual, gain, start):
    NZ, RU, FB, DB, D, CTX = cfg
    NT, RB = NZ * 3 * RU, 3 * RU
    vmem = pl.BlockSpec(memory_space=pltpu.VMEM)
    flops = 8 * NT * CTX * DB
    basis, ab = pl.pallas_call(
        functools.partial(kernel, cfg),
        out_shape=(jax.ShapeDtypeStruct((3, FB, DB), F32), jax.ShapeDtypeStruct((8, LB), F32)),
        in_specs=[pl.BlockSpec(memory_space=pltpu.HBM)] * 4,
        out_specs=(vmem, vmem),
        scratch_shapes=[
            pltpu.VMEM((2, NT, NX * FB), BF16),
            pltpu.VMEM((NZ, RB, DB), BF16),
            pltpu.VMEM((FB, DB), F32),
            pltpu.VMEM((1, DB), F32),
            pltpu.VMEM((ITERS, 2, DB, NX * FB), BF16),
            pltpu.VMEM((DB, NT), F32),
            pltpu.VMEM((DB, NT), F32),
            pltpu.VMEM((8, NT), F32),
            pltpu.VMEM((DB, NT), BF16),
            pltpu.VMEM((ITERS, DB, NX * FB), BF16),
            pltpu.VMEM((ITERS, DB, NX * FB), BF16),
            pltpu.VMEM((4, DB, FB), F32),
            pltpu.VMEM((ITERS, 7, DB, FB), BF16),
            pltpu.VMEM((3, DB, FB), F32),
            pltpu.VMEM((ITERS + 1, 8, 2 * (NT // LB), LB), F32),
            pltpu.VMEM((ITERS + 1, NZ // 2, 2 * (NT // LB), LB), F32),
            pltpu.VMEM((2, 8, LB), F32),
            pltpu.VMEM((2 * NX * NX, 8, LB), F32),
            pltpu.VMEM((NZ, 1, LB), F32),
            pltpu.SemaphoreType.DMA((320,)),
            pltpu.SemaphoreType.DMA((320,)),
            pltpu.SemaphoreType.DMA((4,)),
        ],
        compiler_params=pltpu.CompilerParams(collective_id=0, has_side_effects=True, vmem_limit_bytes=40 * 2 ** 20),
        cost_estimate=pl.CostEstimate(flops=flops, bytes_accessed=2 ** 21, transcendentals=0),
    )(context, residual.reshape(NZ // 2, 2 * RB, DB), gain.reshape(1, DB), start)
    return basis, ab[0:2, 0], ab[2:4, 0]


def solution(mesh):
    cfg = (16, 16, 512, 128, 8192, 4096)
    in_specs = (P("dp", "tensor"), P("tensor", "dp"), P("dp"), P("tensor", "dp"))
    out_specs = (P(None, "tensor", "dp"), P(), P())
    return jax.shard_map(
        functools.partial(body, cfg), mesh=mesh, in_specs=in_specs, out_specs=out_specs, check_vma=False)
```
